256 devices in a mesh: group: 16 (over y_hi, x, core), tensor: 16 (over z, y_lo).
Axes of the slice: x: 4, y: 4 (y_hi: 2, y_lo: 2; y = y_hi * 2 + y_lo), z: 8, core: 2. Of those that a mesh axis runs over, the one named last changes fastest.
Arguments:
- states: bfloat16 [64, 4, 5120], P('group'), may hold values from -38 to 38
- input_gain: bfloat16 [5120], replicated, may hold values from 0.25 to 1.75
- post_gain: bfloat16 [5120], replicated, may hold values from 0.25 to 1.75
- norm_gains: float32 [2, 128], replicated, may hold values from 0.4 to 2.5
- query_weight: bfloat16 [5120, 4096], P(None, 'tensor'), may hold values from -0.078125 to 0.078125
- key_value_weight: bfloat16 [2, 5120, 512], P(None, 'tensor'), may hold values from -0.078125 to 0.078125
- output_weight: bfloat16 [4096, 5120], P('tensor'), may hold values from -0.09375 to 0.09375
- query_down: float32 [5120, 64], P('tensor', 'group'), may hold values from -0.078125 to 0.078125
- query_up: float32 [64, 4096], P('group', 'tensor'), may hold values from -0.24 to 0.24
- pair_down: float32 [2, 5120, 64], P(None, 'tensor', 'group'), may hold values from -0.078125 to 0.078125
- pair_up: float32 [2, 64, 512], P(None, 'group', 'tensor'), may hold values from -0.24 to 0.24
- output_down: float32 [4096, 64], P('tensor', 'group'), may hold values from -0.09375 to 0.09375
- output_up: float32 [64, 5120], P('group', 'tensor'), may hold values from -0.24 to 0.24
- cache_keys: bfloat16 [64, 4096, 512], P('group', 'tensor'), may hold values from -608 to 608
- cache_values: bfloat16 [64, 4096, 512], P('group', 'tensor'), may hold values from -6 to 6
- lengths: int32 [64], P('group'), may hold values from 1024 to 4092, as said below
Outputs:
- residual: bfloat16 [64, 4, 5120], P('group')
- normed: bfloat16 [64, 4, 5120], P('group')
The draws below stay inside these ranges and needn't reach their ends.
Inputs may be any that keep to these rules, and one draw needn't show every extreme that they name: `lengths`: positions of a game at or beyond its length hold no prompt token.
All inputs are finite; a program needn't handle non-finite values.
Results may differ from the reference program's by a relative error of at most 0.006.
The reference program's roundings to bfloat16 on the way count: a program that leaves them out, or rounds other values in their place, can miss the bound.
Values may be sent and summed in bfloat16 or wider, within the bound.
No kernel may reach another device: no remote copies, remote signals or barrier semaphores. Data moves between devices by JAX's collectives and lax.ppermute only.
A program may use at most 64 MiB of HBM per device.

```python
import math
import jax
import jax.numpy as jnp
from jax import lax

D = 5120
HD = 128
QH = 32
KVH = 4
R = 64
STEPS = 4
CACHE = 4096
GAMES_ALL = 64
QW = 4096
KW = 512
BLOCK = 256


def draw_states(key, part):
    key = jax.random.fold_in(key, 11)
    key_rows, key_cols, key_base = jax.random.split(key, 3)
    row_scale = jnp.exp(jax.random.uniform(key_rows, (GAMES_ALL, STEPS, 1), minval=0.0, maxval=math.log(10.0)))
    col_scale = jnp.exp(jax.random.uniform(key_cols, (D,), minval=-0.5 * math.log(10.0), maxval=0.5 * math.log(10.0)))
    base = jnp.clip(jax.random.normal(key_base, (GAMES_ALL, STEPS, D)), -4.0, 4.0)
    return (base * row_scale * col_scale * 0.3).astype(jnp.bfloat16)


def draw_cache_keys(key, part):
    key = jax.random.fold_in(key, 23)
    key_base = jax.random.fold_in(key, 0)
    stored = jnp.clip(jax.random.normal(key_base, (GAMES_ALL, CACHE, KW)), -4.0, 4.0)
    return stored.astype(jnp.bfloat16)


def draw_lengths(key, part):
    key = jax.random.fold_in(key, 37)
    key_draw, key_order = jax.random.split(key, 2)
    shortest = CACHE // 4
    longest = CACHE - STEPS
    drawn = jax.random.randint(key_draw, (GAMES_ALL,), shortest, longest + 1)
    order = jax.random.permutation(key_order, GAMES_ALL)
    drawn = drawn.at[order[0]].set(longest).at[order[1]].set(shortest)
    return drawn.astype(jnp.int32)


def level_of(own_key, shape, cuts, low, high):
    def one(axis_at, shards_of):
        heights = jax.random.uniform(jax.random.fold_in(jax.random.fold_in(own_key, 6), axis_at), (shards_of,), jnp.float32, low / len(cuts), high / len(cuts))
        return jnp.repeat(jnp.exp(heights), shape[axis_at] // shards_of).reshape((-1,) + (1,) * (len(shape) - axis_at - 1))

    gain = one(*cuts[0])
    for cut in cuts[1:]:
        gain = gain * one(*cut)
    return gain


def centred(key, extent, width, bound, shards=(), kind=jnp.bfloat16):
    values = jax.random.normal(key, extent, jnp.float32) * width
    if len(shards) > 0:
        values = level_of(key, extent, shards, -0.22, 0.18) * values
    return jnp.clip(values, min=-bound, max=bound).astype(kind)


def setup_inputs(seed: int = 0) -> dict:
    keys = jax.random.split(jax.random.key(seed), 17)
    return {
        "states": draw_states(jax.random.fold_in(keys[16], 71), 0),
        "input_gain": jnp.clip(1.0 + 0.15 * jax.random.normal(keys[1], (D,), jnp.float32), 0.25, 1.75).astype(jnp.bfloat16),
        "post_gain": jnp.clip(1.0 + 0.15 * jax.random.normal(keys[2], (D,), jnp.float32), 0.25, 1.75).astype(jnp.bfloat16),
        "norm_gains": jnp.clip(jnp.exp(jax.random.uniform(keys[3], (2, HD), jnp.float32, math.log(0.4), math.log(2.5))), 0.4, 2.5),
        "query_weight": centred(keys[4], (D, QW), D ** -0.5, 0.078125, ((1, 16),)),
        "key_value_weight": centred(keys[5], (2, D, KW), D ** -0.5, 0.078125, ((1, 16),)),
        "output_weight": centred(keys[6], (QW, D), QW ** -0.5, 0.09375, ((0, 16),)),
        "query_down": centred(keys[7], (D, R), D ** -0.5, 0.078125, ((0, 16), (1, 16)), jnp.float32),
        "query_up": centred(keys[8], (R, QW), 0.04, 0.24, ((0, 16), (1, 16)), jnp.float32),
        "pair_down": centred(keys[9], (2, D, R), D ** -0.5, 0.078125, ((1, 16), (2, 16)), jnp.float32),
        "pair_up": centred(keys[10], (2, R, KW), 0.04, 0.24, ((1, 16), (2, 16)), jnp.float32),
        "output_down": centred(keys[11], (QW, R), QW ** -0.5, 0.09375, ((0, 16), (1, 16)), jnp.float32),
        "output_up": centred(keys[12], (R, D), 0.04, 0.24, ((0, 16), (1, 16)), jnp.float32),
        "cache_keys": draw_cache_keys(jax.random.fold_in(keys[16], 71), 0),
        "cache_values": centred(keys[14], (GAMES_ALL, CACHE, KW), 1.0, 6.0, ((0, 16), (1, 16))),
        "lengths": draw_lengths(jax.random.fold_in(keys[16], 71), 0),
    }


epsilon = 1e-06
lowrank_adapter_scale = 2.0
rope_theta = 1000000.0
masked_score = -1e+30

def norm_rows(values):
    return values * lax.rsqrt(lax.optimization_barrier(jnp.mean(values * values, axis=-1, keepdims=True)) + epsilon)

def rope_tables(positions, head_size):
    half_size = head_size // 2
    inverse = rope_theta ** (-(jnp.arange(half_size, dtype=jnp.float32) * 2.0 / head_size))
    angles = positions.astype(jnp.float32)[..., None] * inverse
    return (jnp.cos(angles), jnp.sin(angles))

def rotate_half(values, cosine, sine_table):
    half_size = values.shape[-1] // 2
    first_half = values[..., :half_size]
    second_half = values[..., half_size:]
    return jnp.concatenate([first_half * cosine - second_half * sine_table, second_half * cosine + first_half * sine_table], axis=-1)

def merge_factors(frozen_weight_matrix, down_factor, up_factor):
    lowrank_update_term = jnp.dot(down_factor, up_factor, precision=lax.Precision.HIGHEST)
    return (frozen_weight_matrix.astype(jnp.float32) + lowrank_adapter_scale * lowrank_update_term).astype(jnp.bfloat16)

def attend_game(inputs):
    queries, fresh_keys, fresh_values, cache_keys, cache_values, length = inputs
    step_count = queries.shape[0]
    share_count = QH // KVH
    block_count = CACHE // BLOCK
    score_scale = 1.0 / math.sqrt(HD)
    grouped = queries.astype(jnp.float32).reshape(step_count, KVH, share_count, HD)
    block_keys = cache_keys.astype(jnp.float32).reshape(block_count, BLOCK, KVH, HD)
    block_values = cache_values.astype(jnp.float32).reshape(block_count, BLOCK, KVH, HD)
    scores = jnp.einsum('skqd,nbkd->skqnb', grouped, block_keys) * score_scale
    slot_index = jnp.arange(CACHE, dtype=jnp.int32).reshape(block_count, BLOCK)
    valid_mask = slot_index < length
    masked = jnp.where(valid_mask, scores, masked_score)
    block_running_peak = lax.optimization_barrier(jnp.max(masked, axis=-1))
    block_weights = jnp.where(valid_mask, jnp.exp(masked - block_running_peak[..., None]), 0.0)
    block_sum = lax.optimization_barrier(jnp.sum(block_weights, axis=-1))
    rounded = lax.optimization_barrier(block_weights.astype(jnp.bfloat16)).astype(jnp.float32)
    block_acc = jnp.einsum('skqnb,nbkd->skqnd', rounded, block_values)
    fresh_scores = jnp.einsum('skqd,tkd->skqt', grouped, fresh_keys.astype(jnp.float32)) * score_scale
    causal = (jnp.arange(step_count)[:, None] >= jnp.arange(step_count)[None, :])[:, None, None, :]
    fresh_masked = jnp.where(causal, fresh_scores, masked_score)
    fresh_max = lax.optimization_barrier(jnp.max(fresh_masked, axis=-1))
    fresh_weights = jnp.where(causal, jnp.exp(fresh_masked - fresh_max[..., None]), 0.0)
    fresh_sum = lax.optimization_barrier(jnp.sum(fresh_weights, axis=-1))
    fresh_rounded = lax.optimization_barrier(fresh_weights.astype(jnp.bfloat16)).astype(jnp.float32)
    fresh_acc = jnp.einsum('skqt,tkd->skqd', fresh_rounded, fresh_values.astype(jnp.float32))
    highest = jnp.maximum(lax.optimization_barrier(jnp.max(block_running_peak, axis=-1)), fresh_max)
    block_scaling = jnp.exp(block_running_peak - highest[..., None])
    fresh_scaling = jnp.exp(fresh_max - highest)
    total_sum = lax.optimization_barrier(jnp.sum(block_sum * block_scaling, axis=-1)) + fresh_sum * fresh_scaling
    total_acc = lax.optimization_barrier(jnp.sum(block_acc * block_scaling[..., None], axis=3)) + fresh_acc * fresh_scaling[..., None]
    return (total_acc / total_sum[..., None]).astype(jnp.bfloat16).reshape(step_count, QH * HD)

def reference(states, input_gain, post_gain, norm_gains, query_weight, key_value_weight, output_weight, query_down, query_up, pair_down, pair_up, output_down, output_up, cache_keys, cache_values, lengths):
    query_merged = merge_factors(query_weight, query_down, query_up)
    key_merged = merge_factors(key_value_weight[0], pair_down[0], pair_up[0])
    value_merged = merge_factors(key_value_weight[1], pair_down[1], pair_up[1])
    output_merged = merge_factors(output_weight, output_down, output_up)
    game_count, step_count, model_width = states.shape
    activations = states.astype(jnp.float32)
    normed_input = (norm_rows(activations) * input_gain.astype(jnp.float32)).astype(jnp.bfloat16)
    flat_input = normed_input.reshape(game_count * step_count, model_width)
    query_raw = jnp.dot(flat_input, query_merged, preferred_element_type=jnp.float32).reshape(game_count, step_count, QH, HD)
    key_raw = jnp.dot(flat_input, key_merged, preferred_element_type=jnp.float32).reshape(game_count, step_count, KVH, HD)
    value_raw = jnp.dot(flat_input, value_merged, preferred_element_type=jnp.float32).reshape(game_count, step_count, KVH, HD)
    positions = lengths[:, None] + jnp.arange(step_count, dtype=jnp.int32)[None, :]
    cosine, sine_table = rope_tables(positions, HD)
    cosine_heads = cosine[:, :, None, :]
    sine_heads = sine_table[:, :, None, :]
    queries = rotate_half(norm_rows(query_raw) * norm_gains[0], cosine_heads, sine_heads).astype(jnp.bfloat16)
    fresh_keys = rotate_half(norm_rows(key_raw) * norm_gains[1], cosine_heads, sine_heads).astype(jnp.bfloat16)
    fresh_values = value_raw.astype(jnp.bfloat16)
    attended = lax.map(attend_game, (queries, fresh_keys, fresh_values, cache_keys, cache_values, lengths))
    attended = attended.reshape(game_count * step_count, QH * HD)
    projected = jnp.dot(attended, output_merged, preferred_element_type=jnp.float32)
    stream = activations.reshape(game_count * step_count, model_width) + projected
    normed = norm_rows(stream) * post_gain.astype(jnp.float32)
    return (stream.astype(jnp.bfloat16).reshape(states.shape), normed.astype(jnp.bfloat16).reshape(states.shape))
```

```python
import functools
import math

import jax
import jax.numpy as jnp
from jax import lax
from jax.experimental import pallas as pl
from jax.experimental.pallas import tpu as pltpu
from jax.sharding import PartitionSpec as P

HD = 128
QH = 32
KVH = 4
N = 16
ROWS = 16
GAMES = 4
STEPS = 4
RANK = 64
D = 5120
COLS = D // N
WIDE = COLS + RANK
BLOCK = 256

epsilon = 1e-06
rope_theta = 1000000.0
masked_score = -1e30
score_scale = 1.0 / math.sqrt(HD)
HIGHEST = lax.Precision.HIGHEST
f32 = jnp.float32
bf16 = jnp.bfloat16

VMEM = pl.BlockSpec(memory_space=pltpu.VMEM)
SMEM = pl.BlockSpec(memory_space=pltpu.SMEM)


def dot(a, b, contract=((1,), (0,)), precision=None):
    return lax.dot_general(
        a, b, (contract, ((), ())), precision=precision, preferred_element_type=f32
    )


def run(body, outs, args, name, specs=None, scratch=(), flops=0):
    return pl.pallas_call(
        body,
        out_shape=outs,
        in_specs=specs or [VMEM] * len(args),
        out_specs=jax.tree.map(lambda _: VMEM, outs),
        scratch_shapes=list(scratch),
        compiler_params=pltpu.CompilerParams(vmem_limit_bytes=48 << 20),
        name=name,
    )(*args)


def pack_factors(qd, qu, pd, pu, od, ou, out):
    block = jnp.concatenate(
        [
            jnp.concatenate([qd[...], pu[0], pu[1]], axis=1),
            jnp.concatenate([pd[0], jnp.zeros((4, 64), f32)], axis=1),
            jnp.concatenate([pd[1], jnp.zeros((4, 64), f32)], axis=1),
            jnp.concatenate([ou[...], jnp.zeros((4, 64), f32)], axis=1),
            jnp.concatenate([qu[...], jnp.zeros((4, 128), f32)], axis=1),
            jnp.concatenate([od[...], jnp.zeros((4, 128), f32)], axis=1),
        ],
        axis=0,
    )
    for g in range(N):
        out[g] = block


def own_columns(ref, t, rows):
    odd = lax.rem(t, 2)
    start = pl.multiple_of(t * COLS - odd * 64, 128)
    window = ref[:, pl.ds(start, WIDE)]
    return jnp.where(odd == 1, window[:, 64:WIDE], window[:, 0:COLS])


def normalise_input(
    recv, states, gain, kvw, out, x_out, st_out, qu_out, od_out, ou_out, act, xs, ranks, part
):
    t = lax.axis_index("tensor")
    for g in range(GAMES):
        act[4 * g : 4 * g + 4, :] = states[g].astype(f32)
    values = act[...]
    scale = lax.rsqrt(jnp.mean(values * values, axis=-1, keepdims=True) + epsilon)
    x = (values * scale * gain[...]).astype(bf16)
    x_out[...] = x
    xs[...] = x.astype(f32)
    st_out[...] = own_columns(act, t, ROWS)
    xt = own_columns(xs, t, ROWS)
    for g in range(N):
        for j in range(6):
            ranks[j, 4 * g : 4 * g + 4, :] = recv[g, 4 * j : 4 * j + 4, :]
    ou_out[...] = ranks[3, :, 0:COLS]
    qu_out[...] = ranks[4, :, 0:256]
    od_out[...] = ranks[5, :, 0:256]
    xb = xt.astype(bf16)
    for n in range(2):
        base = dot(xb, kvw[n])
        low = dot(xt, ranks[1 + n, :, 0:COLS], ((1,), (1,)), HIGHEST)
        part[:, 512 * n : 512 * n + 512] = base
        part[:, 1024 + 64 * n : 1088 + 64 * n] = low
    shared = ranks[0]
    for d in range(N):
        k, g = d // 4, d % 4
        rows = slice(4 * g, 4 * g + 4)
        out[d, 0:RANK, :] = shared
        out[d, RANK : RANK + 4, 0:128] = part[rows, 128 * k : 128 * k + 128]
        out[d, RANK : RANK + 4, 128:256] = part[rows, 512 + 128 * k : 640 + 128 * k]
        out[d, RANK : RANK + 4, 256:384] = part[rows, 1024:1152]
        out[d, RANK + 4 : RANK + 8, :] = jnp.zeros((4, WIDE), f32)


def rotate(values, cosine, sine):
    return values * cosine + pltpu.roll(values, HD // 2, 1) * sine


def head_norm(values, gain):
    return values * lax.rsqrt(jnp.mean(values * values, axis=-1, keepdims=True) + epsilon) * gain


def merge_queries(recv, qw, x, qu, gains, cos, sin, cos4, sin4, out, fk_out, fv_out):
    t = lax.axis_index("tensor")
    up = qu[...]
    raw = jnp.zeros((ROWS, 256), f32)
    for p in range(N // 2):
        merged = []
        for s in (2 * p, 2 * p + 1):
            update = dot(recv[s, 0:RANK, 0:COLS], up, ((0,), (0,)), HIGHEST)
            merged.append(
                (qw[COLS * s : COLS * s + COLS, :].astype(f32) + 2.0 * update).astype(bf16)
            )
        raw += dot(x[:, 640 * p : 640 * p + 640], jnp.concatenate(merged, axis=0))
    heads = []
    for h in range(2):
        v = head_norm(raw[:, HD * h : HD * h + HD], gains[0:1, :])
        heads.append(rotate(v, cos[...], sin[...]))
    queries = jnp.concatenate(heads, axis=1).astype(bf16)
    for d in range(N):
        out[d] = queries
    total = recv[0, RANK : RANK + 8, :]
    for s in range(1, N):
        total += recv[s, RANK : RANK + 8, :]
    group = 4 * (t // 4)
    keys, values = [], []
    for j in range(4):
        ups = recv[group + j, 0:RANK, COLS:WIDE]
        keys.append(dot(total[:, 256:320], ups[:, 0:32], precision=HIGHEST))
        values.append(dot(total[:, 320:384], ups[:, 32:64], precision=HIGHEST))
    key_raw = total[:, 0:128] + 2.0 * jnp.concatenate(keys, axis=1)
    value_raw = total[:, 128:256] + 2.0 * jnp.concatenate(values, axis=1)
    game = lax.rem(t, 4)
    fk = rotate(head_norm(key_raw, gains[1:2, :]), cos4[game], sin4[game])
    fk_out[...] = fk
    fv_out[...] = value_raw


def attend(lengths, recv, ck, cv, fk, fv, out, qs, ms, ls, accs):
    t = lax.axis_index("tensor")
    row = lax.broadcasted_iota(jnp.int32, (128, 1), 0)
    row_game = lax.rem(row, 16) // 4
    row_step = lax.rem(row, 4)
    length = jnp.zeros((128, 1), jnp.int32)
    for g in range(GAMES):
        length = jnp.where(row_game == g, lengths[g], length)
    slot = t * BLOCK + lax.broadcasted_iota(jnp.int32, (128, BLOCK), 1)
    valid = slot < length
    for k in range(KVH):
        q = jnp.concatenate(
            [recv[4 * k + i, :, HD * j : HD * j + HD] for i in range(4) for j in range(2)], axis=0
        )
        qs[k] = q
        lanes = slice(HD * k, HD * k + HD)
        scores = jnp.zeros((128, BLOCK), f32)
        for g in range(GAMES):
            own = dot(q, ck[g, :, lanes], ((1,), (1,)))
            scores = jnp.where(row_game == g, own, scores)
        scores = jnp.where(valid, scores * score_scale, masked_score)
        peak = jnp.max(scores, axis=-1, keepdims=True)
        weights = jnp.where(valid, jnp.exp(scores - peak), 0.0)
        ms[k] = peak
        ls[k] = jnp.sum(weights, axis=-1, keepdims=True)
        rounded = weights.astype(bf16)
        acc = jnp.zeros((128, HD), f32)
        for g in range(GAMES):
            mine = jnp.where(row_game == g, rounded, jnp.zeros_like(rounded))
            acc += dot(mine, cv[g, :, lanes])
        accs[k] = acc
    kk, game = t // 4, lax.rem(t, 4)
    zeros = jnp.zeros((120, HD), f32)
    keys = jnp.concatenate([fk[...], zeros], axis=0).astype(bf16)
    values = jnp.concatenate([fv[...], zeros], axis=0).astype(bf16)
    fresh = dot(qs[kk], keys, ((1,), (1,))) * score_scale
    later = lax.broadcasted_iota(jnp.int32, (128, 128), 1)
    causal = jnp.logical_and(row_game == game, later <= row_step)
    fresh = jnp.where(causal, fresh, masked_score)
    fresh_peak = jnp.max(fresh, axis=-1, keepdims=True)
    fresh_weights = jnp.where(causal, jnp.exp(fresh - fresh_peak), 0.0)
    fresh_sum = jnp.sum(fresh_weights, axis=-1, keepdims=True)
    fresh_acc = dot(fresh_weights.astype(bf16), values)
    highest = jnp.maximum(ms[kk], fresh_peak)
    old, new = jnp.exp(ms[kk] - highest), jnp.exp(fresh_peak - highest)
    ls[kk] = ls[kk] * old + fresh_sum * new
    accs[kk] = accs[kk] * old + fresh_acc * new
    ms[kk] = highest
    eye = lax.broadcasted_iota(jnp.int32, (128, 128), 0) == later
    for k in range(KVH):
        peaks = jnp.sum(jnp.where(eye, ms[k], 0.0), axis=0, keepdims=True)
        sums = jnp.sum(jnp.where(eye, ls[k], 0.0), axis=0, keepdims=True)
        for i in range(4):
            d = 4 * k + i
            out[d, 0:32, :] = accs[k, 32 * i : 32 * i + 32, :]
            shift = (128 - 32 * i) % 128
            a = pltpu.roll(peaks, shift, 1) if shift else peaks
            b = pltpu.roll(sums, shift, 1) if shift else sums
            out[d, 32:33, :] = a
            out[d, 33:34, :] = b
            out[d, 34:40, :] = jnp.zeros((6, 128), f32)


def project(recv, ow, od, out):
    peaks, sums = recv[:, 32, :], recv[:, 33, :]
    highest = jnp.max(peaks, axis=0, keepdims=True)
    scale = jnp.exp(peaks - highest)
    total = jnp.sum(sums * scale, axis=0, keepdims=True)
    share = scale / total
    share = jnp.concatenate([share, jnp.zeros((112, 128), f32)], axis=0).T
    acc = jnp.zeros((32, HD), f32)
    for s in range(N):
        acc += recv[s, 0:32, :] * share[0:32, s : s + 1]
    joint = jnp.concatenate([acc[0:16], acc[16:32]], axis=1)
    attended = joint.astype(bf16)
    low = dot(attended.astype(f32), od[...], ((1,), (1,)), HIGHEST)
    for p in range(N // 2):
        part = dot(attended, ow[:, 640 * p : 640 * p + 640])
        out[2 * p] = jnp.concatenate([part[:, 0:COLS], low], axis=1)
        out[2 * p + 1] = jnp.concatenate([part[:, COLS:640], low], axis=1)


def add_residual(recv, ou, st, out):
    total = recv[0]
    for s in range(1, N):
        total += recv[s]
    projected = total[:, 0:COLS] + 2.0 * dot(total[:, COLS:WIDE], ou[...], precision=HIGHEST)
    stream = st[...] + projected
    squares = jnp.sum(stream * stream, axis=-1, keepdims=True)
    high = squares.astype(bf16).astype(f32)
    middle = (squares - high).astype(bf16).astype(f32)
    low = squares - high - middle
    lane = lax.broadcasted_iota(jnp.int32, (ROWS, RANK), 1)
    tail = jnp.where(lane == 0, high, 0.0)
    tail = jnp.where(lane == 1, middle, tail)
    tail = jnp.where(lane == 2, low, tail)
    piece = jnp.concatenate([stream, tail], axis=1).astype(bf16)
    for d in range(N):
        out[d] = piece


def finish(recv, gain, residual, normed):
    squares = jnp.zeros((ROWS, RANK), f32)
    for s in range(N):
        squares += recv[s, :, COLS:WIDE].astype(f32)
    mean = jnp.sum(squares, axis=-1, keepdims=True) * (1.0 / D)
    scale = lax.rsqrt(mean + epsilon)
    for p in range(N // 2):
        lanes = slice(640 * p, 640 * p + 640)
        both = jnp.concatenate(
            [recv[2 * p, :, 0:COLS].astype(f32), recv[2 * p + 1, :, 0:COLS].astype(f32)], axis=1
        )
        scaled = both * scale * gain[:, lanes]
        for g in range(GAMES):
            rows = slice(4 * g, 4 * g + 4)
            residual[g, :, lanes] = both[rows].astype(bf16)
            normed[g, :, lanes] = scaled[rows].astype(bf16)


def exchange(array, axis):
    return lax.all_to_all(array, axis, 0, 0, tiled=True)


def rope_tables(lengths):
    positions = lengths[:, None] + jnp.arange(STEPS, dtype=jnp.int32)[None, :]
    inverse = rope_theta ** (-(jnp.arange(HD // 2, dtype=f32) * 2.0 / HD))
    angles = positions.astype(f32)[..., None] * inverse
    cos, sin = jnp.cos(angles), jnp.sin(angles)
    return jnp.concatenate([cos, cos], axis=-1), jnp.concatenate([-sin, sin], axis=-1)


def local(
    states,
    input_gain,
    post_gain,
    norm_gains,
    query_weight,
    key_value_weight,
    output_weight,
    query_down,
    query_up,
    pair_down,
    pair_up,
    output_down,
    output_up,
    cache_keys,
    cache_values,
    lengths,
):
    shape = jax.ShapeDtypeStruct
    cos, sin = rope_tables(lengths)
    factors = run(
        pack_factors,
        shape((N, 24, WIDE), f32),
        (
            query_down.T,
            query_up,
            pair_down.transpose(0, 2, 1),
            pair_up,
            output_down.T,
            output_up,
        ),
        "pack_factors",
    )
    factors = exchange(factors, "group")
    shared, x, own_states, up_query, down_output, up_output = run(
        normalise_input,
        (
            shape((N, RANK + 8, WIDE), f32),
            shape((ROWS, D), bf16),
            shape((ROWS, COLS), f32),
            shape((RANK, 256), f32),
            shape((RANK, 256), f32),
            shape((RANK, COLS), f32),
        ),
        (factors, states, input_gain.astype(f32)[None, :], key_value_weight),
        "normalise_input",
        scratch=[
            pltpu.VMEM((ROWS, D), f32),
            pltpu.VMEM((ROWS, D), f32),
            pltpu.VMEM((6, RANK, WIDE), f32),
            pltpu.VMEM((ROWS, 1152), f32),
        ],
    )
    shared = exchange(shared, "tensor")
    pad = jnp.zeros((GAMES, 4, HD), f32)
    queries, fresh_keys, fresh_values = run(
        merge_queries,
        (shape((N, ROWS, 256), bf16), shape((8, HD), f32), shape((8, HD), f32)),
        (
            shared,
            query_weight,
            x,
            up_query,
            norm_gains,
            cos.reshape(ROWS, HD),
            sin.reshape(ROWS, HD),
            jnp.concatenate([cos, pad], axis=1),
            jnp.concatenate([sin, pad], axis=1),
        ),
        "merge_queries",
    )
    queries = exchange(queries, "tensor")
    partials = run(
        attend,
        shape((N, 40, HD), f32),
        (lengths, queries, cache_keys, cache_values, fresh_keys, fresh_values),
        "attend",
        specs=[SMEM] + [VMEM] * 5,
        scratch=[
            pltpu.VMEM((KVH, 128, HD), bf16),
            pltpu.VMEM((KVH, 128, 1), f32),
            pltpu.VMEM((KVH, 128, 1), f32),
            pltpu.VMEM((KVH, 128, HD), f32),
        ],
    )
    partials = exchange(partials, "tensor")
    projected = run(
        project, shape((N, ROWS, WIDE), f32), (partials, output_weight, down_output), "project"
    )
    projected = exchange(projected, "tensor")
    pieces = run(
        add_residual,
        shape((N, ROWS, WIDE), bf16),
        (projected, up_output, own_states),
        "add_residual",
    )
    pieces = exchange(pieces, "tensor")
    return run(
        finish,
        (shape((GAMES, STEPS, D), bf16), shape((GAMES, STEPS, D), bf16)),
        (pieces, post_gain.astype(f32)[None, :]),
        "finish",
    )


def solution(mesh):
    in_specs = (
        P("group", None, None),
        P(),
        P(),
        P(),
        P(None, "tensor"),
        P(None, "tensor", None),
        P("tensor", None),
        P("tensor", "group"),
        P("group", "tensor"),
        P(None, "tensor", "group"),
        P(None, "group", "tensor"),
        P("tensor", "group"),
        P("group", "tensor"),
        P("group", "tensor", None),
        P("group", "tensor", None),
        P("group"),
    )
    out_specs = (P("group", None, None), P("group", None, None))
    return jax.shard_map(local, mesh=mesh, in_specs=in_specs, out_specs=out_specs, check_vma=False)
```

```python
import functools
import math

import jax
import jax.numpy as jnp
from jax import lax
from jax.experimental import pallas as pl
from jax.experimental.pallas import tpu as pltpu
from jax.sharding import PartitionSpec as P

HD = 128
QH = 32
KVH = 4
N = 16
ROWS = 16
GAMES = 4
STEPS = 4
RANK = 64
D = 5120
COLS = D // N
WIDE = COLS + RANK
BLOCK = 256

epsilon = 1e-06
rope_theta = 1000000.0
masked_score = -1e30
score_scale = 1.0 / math.sqrt(HD)
HIGHEST = lax.Precision.HIGHEST
f32 = jnp.float32
bf16 = jnp.bfloat16

VMEM = pl.BlockSpec(memory_space=pltpu.VMEM)
SMEM = pl.BlockSpec(memory_space=pltpu.SMEM)
HBM = pl.BlockSpec(memory_space=pltpu.HBM)


def dot(a, b, contract=((1,), (0,)), precision=None):
    return lax.dot_general(
        a, b, (contract, ((), ())), precision=precision, preferred_element_type=f32
    )


def run(body, outs, args, name, specs=None, scratch=(), flops=0):
    return pl.pallas_call(
        body,
        out_shape=outs,
        in_specs=specs or [VMEM] * len(args),
        out_specs=jax.tree.map(lambda _: VMEM, outs),
        scratch_shapes=list(scratch),
        compiler_params=pltpu.CompilerParams(vmem_limit_bytes=48 << 20),
        name=name,
    )(*args)


def copies(pairs, sems):
    started = [pltpu.make_async_copy(src, dst, sems.at[i]) for i, (src, dst) in enumerate(pairs)]
    for copy in started:
        copy.start()
    return started


def own_columns(ref, t):
    odd = lax.rem(t, 2)
    start = pl.multiple_of(t * COLS - odd * 64, 128)
    window = ref[:, pl.ds(start, WIDE)]
    return jnp.where(odd == 1, window[:, 64:WIDE], window[:, 0:COLS])


def prepare(
    qd_hbm, pu_hbm, states_hbm, kvw_hbm, gain, out, x_out, xt_out, st_out,
    qd, pu, states, kvw, act, part, sems,
):
    waits = copies(
        [(states_hbm, states), (kvw_hbm, kvw), (qd_hbm, qd), (pu_hbm, pu)], sems
    )
    t = lax.axis_index("tensor")
    waits[0].wait()
    for g in range(GAMES):
        act[4 * g : 4 * g + 4, :] = states[g].astype(f32)
    st_out[...] = own_columns(act, t)
    values = act[...]
    scale = lax.rsqrt(jnp.mean(values * values, axis=-1, keepdims=True) + epsilon)
    x = (values * scale * gain[...]).astype(bf16)
    x_out[...] = x
    act[...] = x.astype(f32)
    xt = own_columns(act, t)
    xt_out[...] = xt
    waits[1].wait()
    for n in range(2):
        part[:, 512 * n : 512 * n + 512] = dot(xt.astype(bf16), kvw[n])
    waits[2].wait()
    waits[3].wait()
    shared = jnp.concatenate([qd[...], pu[0], pu[1]], axis=1)
    for d in range(N):
        k, g = d // 4, d % 4
        rows = slice(4 * g, 4 * g + 4)
        out[d, 0:4, :] = shared
        out[d, 4:8, 0:128] = part[rows, 128 * k : 128 * k + 128]
        out[d, 4:8, 128:256] = part[rows, 512 + 128 * k : 640 + 128 * k]
        out[d, 4:8, 256:384] = jnp.zeros((4, 128), f32)


def regroup(recv, qu_hbm, pd_hbm, od_hbm, ou_hbm, out, base_out, qu, pd, od, ou, sems):
    waits = copies([(qu_hbm, qu), (pd_hbm, pd), (od_hbm, od), (ou_hbm, ou)], sems)
    t = lax.axis_index("tensor")
    base = recv[0]
    for s in range(1, N):
        base += recv[s]
    base_out[...] = base
    for copy in waits:
        copy.wait()
    spare = [qu[:, 64 * c : 64 * c + 64] for c in range(4)]
    spare += [od[:, 64 * c : 64 * c + 64] for c in range(4)]
    spare += [ou[:, 64 * c : 64 * c + 64] for c in range(5)]
    spare += [recv[4 * (t // 4) + c, 0:4, COLS:WIDE] for c in range(4)]
    spare += [jnp.zeros((4, 64), f32)]
    wide = [recv[b, 0:4, 0:COLS] for b in range(N)] + [pd[0], pd[1]]
    blocks = [jnp.concatenate([w, s], axis=1) for w, s in zip(wide, spare)]
    piece = jnp.concatenate(blocks, axis=0)
    for d in range(N):
        out[d] = piece


def rotate(values, cosine, sine):
    return values * cosine + pltpu.roll(values, HD // 2, 1) * sine


def head_norm(values, gain):
    return values * lax.rsqrt(jnp.mean(values * values, axis=-1, keepdims=True) + epsilon) * gain


def split(values):
    high = values.astype(bf16)
    rest = values - high.astype(f32)
    middle = rest.astype(bf16)
    return high, middle, (rest - middle.astype(f32)).astype(bf16)


def merge_queries(
    recv, qw_hbm, x, xt, gains, cos, sin, out, od_out, ou_out, up_out, ranks, qw, sems
):
    chunks = N // 2
    waits = copies(
        [(qw_hbm.at[pl.ds(640 * p, 640)], qw.at[pl.ds(640 * p, 640)]) for p in range(chunks)], sems
    )
    for b in range(18):
        for g in range(N):
            ranks[b, 4 * g : 4 * g + 4, :] = recv[g, 4 * b : 4 * b + 4, :]
    spare = [ranks[b, :, COLS:WIDE] for b in range(17)]
    up = jnp.concatenate(spare[0:4], axis=1)
    od_out[...] = jnp.concatenate(spare[4:8], axis=1)
    ou_out[...] = jnp.concatenate(spare[8:13], axis=1)
    for n in range(2):
        up_out[n] = jnp.concatenate([c[:, 32 * n : 32 * n + 32] for c in spare[13:17]], axis=1)
    uh, um, ul = split(up)
    ups = jnp.concatenate([uh, uh, um, um, ul, uh], axis=0)
    raw = jnp.zeros((ROWS, 256), f32)
    for p in range(chunks):
        waits[p].wait()
        merged = []
        for b in (2 * p, 2 * p + 1):
            h, m, l = split(ranks[b].T[0:COLS])
            hm = jnp.concatenate([h, m], axis=1)
            hl = jnp.concatenate([h, l], axis=1)
            update = dot(jnp.concatenate([hm, hm, hl], axis=1), ups)
            weight = qw[COLS * b : COLS * b + COLS, :].astype(f32)
            merged.append((weight + 2.0 * update).astype(bf16))
        raw += dot(x[:, 640 * p : 640 * p + 640], jnp.concatenate(merged, axis=0))
    heads = []
    for h in range(2):
        v = head_norm(raw[:, HD * h : HD * h + HD], gains[0:1, :])
        heads.append(rotate(v, cos[...], sin[...]))
    queries = jnp.concatenate(heads, axis=1).astype(bf16).astype(f32)
    low = [
        dot(xt[...], ranks[16 + n, :, 0:COLS], ((1,), (1,)), HIGHEST) for n in range(2)
    ]
    low = [part.astype(f32) for part in split(jnp.concatenate(low, axis=1))]
    top = jnp.concatenate(low[0:2], axis=1)
    bottom = jnp.concatenate([low[2], jnp.zeros((ROWS, 128), f32)], axis=1)
    for d in range(N):
        rows = slice(4 * (d % 4), 4 * (d % 4) + 4)
        out[d] = jnp.concatenate([queries, top[rows], bottom[rows]], axis=0).astype(bf16)


def fresh_pair(recv, base, up, gains, cos4, sin4, t):
    total = recv[0, 16:24, :].astype(f32)
    for s in range(1, N):
        total += recv[s, 16:24, :].astype(f32)
    low = total[0:4, 0:128] + total[0:4, 128:256] + total[4:8, 0:128]
    low = jnp.concatenate([low, jnp.zeros((4, 128), f32)], axis=0)
    sums = jnp.concatenate([base[4:8, :], jnp.zeros((4, WIDE), f32)], axis=0)
    keys = sums[:, 0:128] + 2.0 * dot(low[:, 0:64], up[0], precision=HIGHEST)
    values = sums[:, 128:256] + 2.0 * dot(low[:, 64:128], up[1], precision=HIGHEST)
    game = lax.rem(t, 4)
    keys = rotate(head_norm(keys, gains[1:2, :]), cos4[game], sin4[game])
    return keys, values


def attend(lengths, recv, ck, cv, base, up, gains, cos4, sin4, out, qs, ms, ls, accs):
    t = lax.axis_index("tensor")
    fk, fv = fresh_pair(recv, base, up, gains, cos4, sin4, t)
    row = lax.broadcasted_iota(jnp.int32, (128, 1), 0)
    row_game = lax.rem(row, 16) // 4
    row_step = lax.rem(row, 4)
    length = jnp.zeros((128, 1), jnp.int32)
    for g in range(GAMES):
        length = jnp.where(row_game == g, lengths[g], length)
    slot = t * BLOCK + lax.broadcasted_iota(jnp.int32, (128, BLOCK), 1)
    valid = slot < length
    for k in range(KVH):
        q = jnp.concatenate(
            [recv[4 * k + i, 0:ROWS, HD * j : HD * j + HD] for i in range(4) for j in range(2)], axis=0
        )
        qs[k] = q
        lanes = slice(HD * k, HD * k + HD)
        scores = jnp.zeros((128, BLOCK), f32)
        for g in range(GAMES):
            own = dot(q, ck[g, :, lanes], ((1,), (1,)))
            scores = jnp.where(row_game == g, own, scores)
        scores = jnp.where(valid, scores * score_scale, masked_score)
        peak = jnp.max(scores, axis=-1, keepdims=True)
        weights = jnp.where(valid, jnp.exp(scores - peak), 0.0)
        ms[k] = peak
        ls[k] = jnp.sum(weights, axis=-1, keepdims=True)
        rounded = weights.astype(bf16)
        acc = jnp.zeros((128, HD), f32)
        for g in range(GAMES):
            mine = jnp.where(row_game == g, rounded, jnp.zeros_like(rounded))
            acc += dot(mine, cv[g, :, lanes])
        accs[k] = acc
    kk, game = t // 4, lax.rem(t, 4)
    zeros = jnp.zeros((120, HD), f32)
    keys = jnp.concatenate([fk, zeros], axis=0).astype(bf16)
    values = jnp.concatenate([fv, zeros], axis=0).astype(bf16)
    fresh = dot(qs[kk], keys, ((1,), (1,))) * score_scale
    later = lax.broadcasted_iota(jnp.int32, (128, 128), 1)
    causal = jnp.logical_and(row_game == game, later <= row_step)
    fresh = jnp.where(causal, fresh, masked_score)
    fresh_peak = jnp.max(fresh, axis=-1, keepdims=True)
    fresh_weights = jnp.where(causal, jnp.exp(fresh - fresh_peak), 0.0)
    fresh_sum = jnp.sum(fresh_weights, axis=-1, keepdims=True)
    fresh_acc = dot(fresh_weights.astype(bf16), values)
    highest = jnp.maximum(ms[kk], fresh_peak)
    old, new = jnp.exp(ms[kk] - highest), jnp.exp(fresh_peak - highest)
    ls[kk] = ls[kk] * old + fresh_sum * new
    accs[kk] = accs[kk] * old + fresh_acc * new
    ms[kk] = highest
    eye = lax.broadcasted_iota(jnp.int32, (128, 128), 0) == later
    for k in range(KVH):
        peaks = jnp.sum(jnp.where(eye, ms[k], 0.0), axis=0, keepdims=True)
        sums = jnp.sum(jnp.where(eye, ls[k], 0.0), axis=0, keepdims=True)
        for i in range(4):
            d = 4 * k + i
            out[d, 0:32, :] = accs[k, 32 * i : 32 * i + 32, :]
            shift = (128 - 32 * i) % 128
            a = pltpu.roll(peaks, shift, 1) if shift else peaks
            b = pltpu.roll(sums, shift, 1) if shift else sums
            out[d, 32:33, :] = a
            out[d, 33:34, :] = b
            out[d, 34:40, :] = jnp.zeros((6, 128), f32)


def project(recv, ow, od, out):
    peaks, sums = recv[:, 32, :], recv[:, 33, :]
    highest = jnp.max(peaks, axis=0, keepdims=True)
    scale = jnp.exp(peaks - highest)
    total = jnp.sum(sums * scale, axis=0, keepdims=True)
    share = scale / total
    share = jnp.concatenate([share, jnp.zeros((112, 128), f32)], axis=0).T
    acc = jnp.zeros((32, HD), f32)
    for s in range(N):
        acc += recv[s, 0:32, :] * share[0:32, s : s + 1]
    joint = jnp.concatenate([acc[0:16], acc[16:32]], axis=1)
    attended = joint.astype(bf16)
    low = dot(attended.astype(f32), od[...], ((1,), (1,)), HIGHEST)
    for p in range(N // 2):
        part = dot(attended, ow[:, 640 * p : 640 * p + 640])
        out[2 * p] = jnp.concatenate([part[:, 0:COLS], low], axis=1)
        out[2 * p + 1] = jnp.concatenate([part[:, COLS:640], low], axis=1)


def add_residual(recv, ou, st, out):
    total = recv[0]
    for s in range(1, N):
        total += recv[s]
    projected = total[:, 0:COLS] + 2.0 * dot(total[:, COLS:WIDE], ou[...], precision=HIGHEST)
    stream = st[...] + projected
    squares = jnp.sum(stream * stream, axis=-1, keepdims=True)
    high = squares.astype(bf16).astype(f32)
    middle = (squares - high).astype(bf16).astype(f32)
    low = squares - high - middle
    lane = lax.broadcasted_iota(jnp.int32, (ROWS, RANK), 1)
    tail = jnp.where(lane == 0, high, 0.0)
    tail = jnp.where(lane == 1, middle, tail)
    tail = jnp.where(lane == 2, low, tail)
    piece = jnp.concatenate([stream, tail], axis=1).astype(bf16)
    for d in range(N):
        out[d] = piece


def finish(recv, gain, residual, normed):
    squares = jnp.zeros((ROWS, RANK), f32)
    for s in range(N):
        squares += recv[s, :, COLS:WIDE].astype(f32)
    mean = jnp.sum(squares, axis=-1, keepdims=True) * (1.0 / D)
    scale = lax.rsqrt(mean + epsilon)
    for p in range(N // 2):
        lanes = slice(640 * p, 640 * p + 640)
        both = jnp.concatenate(
            [recv[2 * p, :, 0:COLS].astype(f32), recv[2 * p + 1, :, 0:COLS].astype(f32)], axis=1
        )
        scaled = both * scale * gain[:, lanes]
        for g in range(GAMES):
            rows = slice(4 * g, 4 * g + 4)
            residual[g, :, lanes] = both[rows].astype(bf16)
            normed[g, :, lanes] = scaled[rows].astype(bf16)


def exchange(array, axis):
    return lax.all_to_all(array, axis, 0, 0, tiled=True)


def rope_tables(lengths):
    positions = lengths[:, None] + jnp.arange(STEPS, dtype=jnp.int32)[None, :]
    inverse = rope_theta ** (-(jnp.arange(HD // 2, dtype=f32) * 2.0 / HD))
    angles = positions.astype(f32)[..., None] * inverse
    cos, sin = jnp.cos(angles), jnp.sin(angles)
    return jnp.concatenate([cos, cos], axis=-1), jnp.concatenate([-sin, sin], axis=-1)


def local(
    states,
    input_gain,
    post_gain,
    norm_gains,
    query_weight,
    key_value_weight,
    output_weight,
    query_down,
    query_up,
    pair_down,
    pair_up,
    output_down,
    output_up,
    cache_keys,
    cache_values,
    lengths,
):
    shape = jax.ShapeDtypeStruct
    cos, sin = rope_tables(lengths)
    dma = pltpu.SemaphoreType.DMA
    shared, x, own_x, own_states = run(
        prepare,
        (
            shape((N, 8, WIDE), f32),
            shape((ROWS, D), bf16),
            shape((ROWS, COLS), f32),
            shape((ROWS, COLS), f32),
        ),
        (
            query_down.T,
            pair_up,
            states,
            key_value_weight,
            input_gain.astype(f32)[None, :],
        ),
        "prepare",
        specs=[HBM] * 4 + [VMEM],
        scratch=[
            pltpu.VMEM((4, COLS), f32),
            pltpu.VMEM((2, 4, 32), f32),
            pltpu.VMEM((GAMES, STEPS, D), bf16),
            pltpu.VMEM((2, COLS, 512), bf16),
            pltpu.VMEM((ROWS, D), f32),
            pltpu.VMEM((ROWS, 1024), f32),
            dma((4,)),
        ],
    )
    shared = exchange(shared, "tensor")
    factors, base = run(
        regroup,
        (shape((N, 72, WIDE), f32), shape((8, WIDE), f32)),
        (shared, query_up, pair_down.transpose(0, 2, 1), output_down.T, output_up),
        "regroup",
        specs=[VMEM] + [HBM] * 4,
        scratch=[
            pltpu.VMEM((4, 256), f32),
            pltpu.VMEM((2, 4, COLS), f32),
            pltpu.VMEM((4, 256), f32),
            pltpu.VMEM((4, COLS), f32),
            dma((4,)),
        ],
    )
    factors = exchange(factors, "group")
    queries, down_output, up_output, up_pair = run(
        merge_queries,
        (
            shape((N, 24, 256), bf16),
            shape((RANK, 256), f32),
            shape((RANK, COLS), f32),
            shape((2, RANK, HD), f32),
        ),
        (
            factors,
            query_weight,
            x,
            own_x,
            norm_gains,
            cos.reshape(ROWS, HD),
            sin.reshape(ROWS, HD),
        ),
        "merge_queries",
        specs=[VMEM, HBM] + [VMEM] * 5,
        scratch=[
            pltpu.VMEM((18, RANK, WIDE), f32),
            pltpu.VMEM((D, 256), bf16),
            dma((N // 2,)),
        ],
    )
    queries = exchange(queries, "tensor")
    pad = jnp.zeros((GAMES, 4, HD), f32)
    partials = run(
        attend,
        shape((N, 40, HD), f32),
        (
            lengths,
            queries,
            cache_keys,
            cache_values,
            base,
            up_pair,
            norm_gains,
            jnp.concatenate([cos, pad], axis=1),
            jnp.concatenate([sin, pad], axis=1),
        ),
        "attend",
        specs=[SMEM] + [VMEM] * 8,
        scratch=[
            pltpu.VMEM((KVH, 128, HD), bf16),
            pltpu.VMEM((KVH, 128, 1), f32),
            pltpu.VMEM((KVH, 128, 1), f32),
            pltpu.VMEM((KVH, 128, HD), f32),
        ],
    )
    partials = exchange(partials, "tensor")
    projected = run(
        project, shape((N, ROWS, WIDE), f32), (partials, output_weight, down_output), "project"
    )
    projected = exchange(projected, "tensor")
    pieces = run(
        add_residual,
        shape((N, ROWS, WIDE), bf16),
        (projected, up_output, own_states),
        "add_residual",
    )
    pieces = exchange(pieces, "tensor")
    return run(
        finish,
        (shape((GAMES, STEPS, D), bf16), shape((GAMES, STEPS, D), bf16)),
        (pieces, post_gain.astype(f32)[None, :]),
        "finish",
    )


def solution(mesh):
    in_specs = (
        P("group", None, None),
        P(),
        P(),
        P(),
        P(None, "tensor"),
        P(None, "tensor", None),
        P("tensor", None),
        P("tensor", "group"),
        P("group", "tensor"),
        P(None, "tensor", "group"),
        P(None, "group", "tensor"),
        P("tensor", "group"),
        P("group", "tensor"),
        P("group", "tensor", None),
        P("group", "tensor", None),
        P("group"),
    )
    out_specs = (P("group", None, None), P("group", None, None))
    return jax.shard_map(local, mesh=mesh, in_specs=in_specs, out_specs=out_specs, check_vma=False)
```

```python
import functools
import math

import jax
import jax.numpy as jnp
from jax import lax
from jax.experimental import pallas as pl
from jax.experimental.pallas import tpu as pltpu
from jax.sharding import PartitionSpec as P

HD = 128
QH = 32
KVH = 4
N = 16
ROWS = 16
GAMES = 4
STEPS = 4
RANK = 64
D = 5120
COLS = D // N
WIDE = COLS + RANK
BLOCK = 256
FULL = D + 1792
HALF = FULL // 2

epsilon = 1e-06
rope_theta = 1000000.0
masked_score = -1e30
score_scale = 1.0 / math.sqrt(HD)
HIGHEST = lax.Precision.HIGHEST
f32 = jnp.float32
bf16 = jnp.bfloat16

VMEM = pl.BlockSpec(memory_space=pltpu.VMEM)
SMEM = pl.BlockSpec(memory_space=pltpu.SMEM)
HBM = pl.BlockSpec(memory_space=pltpu.HBM)


def dot(a, b, contract=((1,), (0,)), precision=None):
    return lax.dot_general(
        a, b, (contract, ((), ())), precision=precision, preferred_element_type=f32
    )


def run(body, outs, args, name, specs=None, scratch=(), limit=48 << 20):
    return pl.pallas_call(
        body,
        out_shape=outs,
        in_specs=specs or [VMEM] * len(args),
        out_specs=jax.tree.map(lambda _: VMEM, outs),
        scratch_shapes=list(scratch),
        compiler_params=pltpu.CompilerParams(vmem_limit_bytes=limit),
        name=name,
    )(*args)


def copies(pairs, sems):
    started = [pltpu.make_async_copy(src, dst, sems.at[i]) for i, (src, dst) in enumerate(pairs)]
    for copy in started:
        copy.start()
    return started


def own_columns(ref, t):
    odd = lax.rem(t, 2)
    start = pl.multiple_of(t * COLS - odd * 64, 128)
    window = ref[:, pl.ds(start, WIDE)]
    return jnp.where(odd == 1, window[:, 64:WIDE], window[:, 0:COLS])


def prepare(
    qd_hbm, pu_hbm, states_hbm, kvw_hbm, gain_hbm, out, x_out, xt_out, st_out,
    qd, pu, states, kvw, gain, act, part, sems,
):
    waits = copies(
        [
            (states_hbm, states),
            (gain_hbm, gain),
            (kvw_hbm, kvw),
            (qd_hbm, qd),
            (pu_hbm, pu),
        ],
        sems,
    )
    t = lax.axis_index("tensor")
    waits[0].wait()
    for g in range(GAMES):
        act[4 * g : 4 * g + 4, :] = states[g].astype(f32)
    st_out[...] = own_columns(act, t)
    values = act[...]
    scale = lax.rsqrt(jnp.mean(values * values, axis=-1, keepdims=True) + epsilon)
    waits[1].wait()
    gains = gain[...].astype(f32)
    for c in range(D // 128):
        lanes = slice(128 * c, 128 * c + 128)
        x = (values[:, lanes] * scale * gains[c : c + 1, :]).astype(bf16)
        x_out[:, lanes] = x
        act[:, lanes] = x.astype(f32)
    xt = own_columns(act, t)
    xt_out[...] = xt
    waits[2].wait()
    for n in range(2):
        part[:, 512 * n : 512 * n + 512] = dot(xt.astype(bf16), kvw[n])
    for copy in waits[3:]:
        copy.wait()
    shared = jnp.concatenate([qd[...], pu[0], pu[1]], axis=1)
    for d in range(N):
        k, g = d // 4, d % 4
        rows = slice(4 * g, 4 * g + 4)
        out[d, 0:4, :] = shared
        out[d, 4:8, 0:128] = part[rows, 128 * k : 128 * k + 128]
        out[d, 4:8, 128:256] = part[rows, 512 + 128 * k : 640 + 128 * k]
        out[d, 4:8, 256:384] = jnp.zeros((4, 128), f32)


def regroup(recv, own, out, base_out, line):
    t = lax.axis_index("tensor")
    base = recv[0]
    for s in range(1, N):
        base += recv[s]
    base_out[...] = base
    for p in range(N // 2):
        line[:, 640 * p : 640 * p + 640] = jnp.concatenate(
            [recv[2 * p, 0:4, 0:COLS], recv[2 * p + 1, 0:4, 0:COLS]], axis=1
        )
    line[:, D : D + 1536] = own[...]
    pairs = [recv[4 * (t // 4) + c, 0:4, COLS:WIDE] for c in range(4)]
    line[:, D + 1536 : FULL] = jnp.concatenate(
        [c[:, 32 * n : 32 * n + 32] for n in range(2) for c in pairs], axis=1
    )
    for d in range(N):
        out[d] = line[:, HALF * (d % 2) : HALF * (d % 2) + HALF]


def assemble(recv, out):
    for c in range(2):
        for g in range(N):
            out[c, 4 * g : 4 * g + 4, :] = recv[g]


def columns(recv, start, width):
    if start + width <= HALF:
        return recv[0, :, start : start + width]
    if start >= HALF:
        return recv[1, :, start - HALF : start - HALF + width]
    left = recv[0, :, start:HALF]
    return jnp.concatenate([left, recv[1, :, 0 : start + width - HALF]], axis=1)


def rotate(values, cosine, sine):
    return values * cosine + pltpu.roll(values, HD // 2, 1) * sine


def head_norm(values, gain):
    return values * lax.rsqrt(jnp.mean(values * values, axis=-1, keepdims=True) + epsilon) * gain


def split(values):
    high = values.astype(bf16)
    rest = values - high.astype(f32)
    middle = rest.astype(bf16)
    return high, middle, (rest - middle.astype(f32)).astype(bf16)


def merge_queries(recv, qwt, x, xt, gains, cos, sin, out, od_out, ou_out, up_out):
    od_out[...] = columns(recv, 6016, 256)
    ou_out[...] = columns(recv, 6272, COLS)
    for n in range(2):
        up_out[n] = columns(recv, 6656 + 128 * n, 128)
    uh, um, ul = [u.astype(f32) for u in split(columns(recv, 5760, 256))]
    ups = jnp.concatenate([uh, uh, um, um, ul, uh], axis=0).T.astype(bf16)
    raw = jnp.zeros((ROWS, 256), f32)
    for p in range(N // 2):
        lanes = slice(640 * p, 640 * p + 640)
        h, m, l = split(columns(recv, 640 * p, 640))
        update = dot(ups, jnp.concatenate([h, m, h, m, h, l], axis=0))
        merged = (qwt[:, lanes].astype(f32) + 2.0 * update).astype(bf16)
        raw += dot(x[:, lanes], merged, ((1,), (1,)))
    cosine = jnp.concatenate([cos[g] for g in range(GAMES)], axis=0)
    sine = jnp.concatenate([sin[g] for g in range(GAMES)], axis=0)
    heads = []
    for h in range(2):
        v = head_norm(raw[:, HD * h : HD * h + HD], gains[0:1, :])
        heads.append(rotate(v, cosine, sine))
    queries = jnp.concatenate(heads, axis=1).astype(bf16).astype(f32)
    low = [
        dot(xt[...], columns(recv, D + COLS * n, COLS), ((1,), (1,)), HIGHEST)
        for n in range(2)
    ]
    low = [part.astype(f32) for part in split(jnp.concatenate(low, axis=1))]
    top = jnp.concatenate(low[0:2], axis=1)
    bottom = jnp.concatenate([low[2], jnp.zeros((ROWS, 128), f32)], axis=1)
    for d in range(N):
        rows = slice(4 * (d % 4), 4 * (d % 4) + 4)
        out[d] = jnp.concatenate([queries, top[rows], bottom[rows]], axis=0).astype(bf16)


def fresh_pair(recv, base, up, gains, cos4, sin4, t):
    total = recv[0, 16:24, :].astype(f32)
    for s in range(1, N):
        total += recv[s, 16:24, :].astype(f32)
    low = total[0:4, 0:128] + total[0:4, 128:256] + total[4:8, 0:128]
    low = jnp.concatenate([low, jnp.zeros((4, 128), f32)], axis=0)
    sums = jnp.concatenate([base[4:8, :], jnp.zeros((4, WIDE), f32)], axis=0)
    keys = sums[:, 0:128] + 2.0 * dot(low[:, 0:64], up[0], precision=HIGHEST)
    values = sums[:, 128:256] + 2.0 * dot(low[:, 64:128], up[1], precision=HIGHEST)
    game = lax.rem(t, 4)
    zeros = jnp.zeros((4, HD), f32)
    cosine = jnp.concatenate([cos4[game], zeros], axis=0)
    sine = jnp.concatenate([sin4[game], zeros], axis=0)
    keys = rotate(head_norm(keys, gains[1:2, :]), cosine, sine)
    return keys, values


def attend(lengths, recv, ck, cv, base, up, gains, cos4, sin4, out, qs, ms, ls, accs):
    t = lax.axis_index("tensor")
    fk, fv = fresh_pair(recv, base, up, gains, cos4, sin4, t)
    row = lax.broadcasted_iota(jnp.int32, (128, 1), 0)
    row_game = lax.rem(row, 16) // 4
    row_step = lax.rem(row, 4)
    length = jnp.zeros((128, 1), jnp.int32)
    for g in range(GAMES):
        length = jnp.where(row_game == g, lengths[g], length)
    slot = t * BLOCK + lax.broadcasted_iota(jnp.int32, (128, BLOCK), 1)
    valid = slot < length
    for k in range(KVH):
        q = jnp.concatenate(
            [recv[4 * k + i, 0:ROWS, HD * j : HD * j + HD] for i in range(4) for j in range(2)], axis=0
        )
        qs[k] = q
        lanes = slice(HD * k, HD * k + HD)
        scores = jnp.zeros((128, BLOCK), f32)
        for g in range(GAMES):
            own = dot(q, ck[g, :, lanes], ((1,), (1,)))
            scores = jnp.where(row_game == g, own, scores)
        scores = jnp.where(valid, scores * score_scale, masked_score)
        peak = jnp.max(scores, axis=-1, keepdims=True)
        weights = jnp.where(valid, jnp.exp(scores - peak), 0.0)
        ms[k] = peak
        ls[k] = jnp.sum(weights, axis=-1, keepdims=True)
        rounded = weights.astype(bf16)
        acc = jnp.zeros((128, HD), f32)
        for g in range(GAMES):
            mine = jnp.where(row_game == g, rounded, jnp.zeros_like(rounded))
            acc += dot(mine, cv[g, :, lanes])
        accs[k] = acc
    kk, game = t // 4, lax.rem(t, 4)
    zeros = jnp.zeros((120, HD), f32)
    keys = jnp.concatenate([fk, zeros], axis=0).astype(bf16)
    values = jnp.concatenate([fv, zeros], axis=0).astype(bf16)
    fresh = dot(qs[kk], keys, ((1,), (1,))) * score_scale
    later = lax.broadcasted_iota(jnp.int32, (128, 128), 1)
    causal = jnp.logical_and(row_game == game, later <= row_step)
    fresh = jnp.where(causal, fresh, masked_score)
    fresh_peak = jnp.max(fresh, axis=-1, keepdims=True)
    fresh_weights = jnp.where(causal, jnp.exp(fresh - fresh_peak), 0.0)
    fresh_sum = jnp.sum(fresh_weights, axis=-1, keepdims=True)
    fresh_acc = dot(fresh_weights.astype(bf16), values)
    highest = jnp.maximum(ms[kk], fresh_peak)
    old, new = jnp.exp(ms[kk] - highest), jnp.exp(fresh_peak - highest)
    ls[kk] = ls[kk] * old + fresh_sum * new
    accs[kk] = accs[kk] * old + fresh_acc * new
    ms[kk] = highest
    eye = lax.broadcasted_iota(jnp.int32, (128, 128), 0) == later
    for k in range(KVH):
        peaks = jnp.sum(jnp.where(eye, ms[k], 0.0), axis=0, keepdims=True)
        sums = jnp.sum(jnp.where(eye, ls[k], 0.0), axis=0, keepdims=True)
        for i in range(4):
            d = 4 * k + i
            out[d, 0:32, :] = accs[k, 32 * i : 32 * i + 32, :]
            shift = (128 - 32 * i) % 128
            a = pltpu.roll(peaks, shift, 1) if shift else peaks
            b = pltpu.roll(sums, shift, 1) if shift else sums
            out[d, 32:33, :] = a
            out[d, 33:34, :] = b
            out[d, 34:40, :] = jnp.zeros((6, 128), f32)


def project(recv, ow, od, out):
    peaks, sums = recv[:, 32, :], recv[:, 33, :]
    highest = jnp.max(peaks, axis=0, keepdims=True)
    scale = jnp.exp(peaks - highest)
    total = jnp.sum(sums * scale, axis=0, keepdims=True)
    share = scale / total
    share = jnp.concatenate([share, jnp.zeros((112, 128), f32)], axis=0).T
    acc = jnp.zeros((32, HD), f32)
    for s in range(N):
        acc += recv[s, 0:32, :] * share[0:32, s : s + 1]
    joint = jnp.concatenate([acc[0:16], acc[16:32]], axis=1)
    attended = joint.astype(bf16)
    low = dot(attended.astype(f32), od[...], ((1,), (1,)), HIGHEST)
    for p in range(N // 2):
        part = dot(attended, ow[:, 640 * p : 640 * p + 640])
        out[2 * p] = jnp.concatenate([part[:, 0:COLS], low], axis=1)
        out[2 * p + 1] = jnp.concatenate([part[:, COLS:640], low], axis=1)


def add_residual(recv, ou, st, out):
    total = recv[0]
    for s in range(1, N):
        total += recv[s]
    projected = total[:, 0:COLS] + 2.0 * dot(total[:, COLS:WIDE], ou[...], precision=HIGHEST)
    stream = st[...] + projected
    squares = jnp.sum(stream * stream, axis=-1, keepdims=True)
    high = squares.astype(bf16).astype(f32)
    middle = (squares - high).astype(bf16).astype(f32)
    low = squares - high - middle
    lane = lax.broadcasted_iota(jnp.int32, (ROWS, RANK), 1)
    tail = jnp.where(lane == 0, high, 0.0)
    tail = jnp.where(lane == 1, middle, tail)
    tail = jnp.where(lane == 2, low, tail)
    piece = jnp.concatenate([stream, tail], axis=1).astype(bf16)
    for d in range(N):
        out[d] = piece


def finish(recv, gain, residual, normed):
    squares = jnp.zeros((ROWS, RANK), f32)
    for s in range(N):
        squares += recv[s, :, COLS:WIDE].astype(f32)
    mean = jnp.sum(squares, axis=-1, keepdims=True) * (1.0 / D)
    scale = lax.rsqrt(mean + epsilon)
    gains = gain[...].astype(f32)
    for p in range(N // 2):
        lanes = slice(640 * p, 640 * p + 640)
        both = jnp.concatenate(
            [recv[2 * p, :, 0:COLS].astype(f32), recv[2 * p + 1, :, 0:COLS].astype(f32)], axis=1
        )
        own = jnp.concatenate([gains[5 * p + c : 5 * p + c + 1, :] for c in range(5)], axis=1)
        scaled = both * scale * own
        for g in range(GAMES):
            rows = slice(4 * g, 4 * g + 4)
            residual[g, :, lanes] = both[rows].astype(bf16)
            normed[g, :, lanes] = scaled[rows].astype(bf16)


def exchange(array, axis):
    return lax.all_to_all(array, axis, 0, 0, tiled=True)


def rope_tables(lengths):
    positions = lengths[:, None] + jnp.arange(STEPS, dtype=jnp.int32)[None, :]
    inverse = rope_theta ** (-(jnp.arange(HD // 2, dtype=f32) * 2.0 / HD))
    angles = positions.astype(f32)[..., None] * inverse
    cos, sin = jnp.cos(angles), jnp.sin(angles)
    return jnp.concatenate([cos, cos], axis=-1), jnp.concatenate([-sin, sin], axis=-1)


def local(
    states,
    input_gain,
    post_gain,
    norm_gains,
    query_weight,
    key_value_weight,
    output_weight,
    query_down,
    query_up,
    pair_down,
    pair_up,
    output_down,
    output_up,
    cache_keys,
    cache_values,
    lengths,
):
    shape = jax.ShapeDtypeStruct
    cos, sin = rope_tables(lengths)
    dma = pltpu.SemaphoreType.DMA
    shared, x, own_x, own_states = run(
        prepare,
        (
            shape((N, 8, WIDE), f32),
            shape((ROWS, D), bf16),
            shape((ROWS, COLS), f32),
            shape((ROWS, COLS), f32),
        ),
        (
            query_down.T,
            pair_up,
            states,
            key_value_weight,
            input_gain.reshape(D // 128, 128),
        ),
        "prepare",
        specs=[HBM] * 5,
        limit=60 << 20,
        scratch=[
            pltpu.VMEM((4, COLS), f32),
            pltpu.VMEM((2, 4, 32), f32),
            pltpu.VMEM((GAMES, STEPS, D), bf16),
            pltpu.VMEM((2, COLS, 512), bf16),
            pltpu.VMEM((D // 128, 128), bf16),
            pltpu.VMEM((ROWS, D), f32),
            pltpu.VMEM((ROWS, 1024), f32),
            dma((5,)),
        ],
    )
    own = jnp.concatenate(
        [
            pair_down[0].T,
            pair_down[1].T,
            query_up,
            output_down.T,
            output_up,
            jnp.zeros((4, 64), f32),
        ],
        axis=1,
    )
    shared, own, cos, sin, query_turned = lax.optimization_barrier(
        (exchange(shared, "tensor"), own, cos, sin, query_weight.T)
    )
    factors, base = run(
        regroup,
        (shape((N, 4, HALF), f32), shape((8, WIDE), f32)),
        (shared, own),
        "regroup",
        scratch=[pltpu.VMEM((4, FULL), f32)],
    )
    factors = exchange(factors, "group")
    factors = run(assemble, shape((2, RANK, HALF), f32), (factors,), "assemble")
    pairs = [[2 * i, 2 * i + 1] for i in range(N // 2)]
    factors = lax.all_to_all(factors, "group", 0, 0, tiled=True, axis_index_groups=pairs)
    queries, down_output, up_output, up_pair = run(
        merge_queries,
        (
            shape((N, 24, 256), bf16),
            shape((RANK, 256), f32),
            shape((RANK, COLS), f32),
            shape((2, RANK, HD), f32),
        ),
        (factors, query_turned, x, own_x, norm_gains, cos, sin),
        "merge_queries",
    )
    queries = exchange(queries, "tensor")
    partials = run(
        attend,
        shape((N, 40, HD), f32),
        (
            lengths,
            queries,
            cache_keys,
            cache_values,
            base,
            up_pair,
            norm_gains,
            cos,
            sin,
        ),
        "attend",
        specs=[SMEM] + [VMEM] * 8,
        scratch=[
            pltpu.VMEM((KVH, 128, HD), bf16),
            pltpu.VMEM((KVH, 128, 1), f32),
            pltpu.VMEM((KVH, 128, 1), f32),
            pltpu.VMEM((KVH, 128, HD), f32),
        ],
    )
    partials = exchange(partials, "tensor")
    projected = run(
        project, shape((N, ROWS, WIDE), f32), (partials, output_weight, down_output), "project"
    )
    projected = exchange(projected, "tensor")
    pieces = run(
        add_residual,
        shape((N, ROWS, WIDE), bf16),
        (projected, up_output, own_states),
        "add_residual",
    )
    pieces = exchange(pieces, "tensor")
    return run(
        finish,
        (shape((GAMES, STEPS, D), bf16), shape((GAMES, STEPS, D), bf16)),
        (pieces, post_gain.reshape(D // 128, 128)),
        "finish",
    )


def solution(mesh):
    in_specs = (
        P("group", None, None),
        P(),
        P(),
        P(),
        P(None, "tensor"),
        P(None, "tensor", None),
        P("tensor", None),
        P("tensor", "group"),
        P("group", "tensor"),
        P(None, "tensor", "group"),
        P(None, "group", "tensor"),
        P("tensor", "group"),
        P("group", "tensor"),
        P("group", "tensor", None),
        P("group", "tensor", None),
        P("group"),
    )
    out_specs = (P("group", None, None), P("group", None, None))
    return jax.shard_map(local, mesh=mesh, in_specs=in_specs, out_specs=out_specs, check_vma=False)
```

```python
import functools
import math

import jax
import jax.numpy as jnp
from jax import lax
from jax.experimental import pallas as pl
from jax.experimental.pallas import tpu as pltpu
from jax.sharding import PartitionSpec as P

HD = 128
QH = 32
KVH = 4
N = 16
ROWS = 16
GAMES = 4
STEPS = 4
RANK = 64
D = 5120
COLS = D // N
WIDE = COLS + RANK
BLOCK = 256
FULL = D + 1792
HALF = FULL // 2

epsilon = 1e-06
rope_theta = 1000000.0
masked_score = -1e30
score_scale = 1.0 / math.sqrt(HD)
HIGHEST = lax.Precision.HIGHEST
f32 = jnp.float32
bf16 = jnp.bfloat16

VMEM = pl.BlockSpec(memory_space=pltpu.VMEM)
SMEM = pl.BlockSpec(memory_space=pltpu.SMEM)
HBM = pl.BlockSpec(memory_space=pltpu.HBM)


def dot(a, b, contract=((1,), (0,)), precision=None):
    return lax.dot_general(
        a, b, (contract, ((), ())), precision=precision, preferred_element_type=f32
    )


def run(body, outs, args, name, specs=None, scratch=(), limit=48 << 20):
    return pl.pallas_call(
        body,
        out_shape=outs,
        in_specs=specs or [VMEM] * len(args),
        out_specs=jax.tree.map(lambda _: VMEM, outs),
        scratch_shapes=list(scratch),
        compiler_params=pltpu.CompilerParams(vmem_limit_bytes=limit),
        name=name,
    )(*args)


def copies(pairs, sems):
    started = [pltpu.make_async_copy(src, dst, sems.at[i]) for i, (src, dst) in enumerate(pairs)]
    for copy in started:
        copy.start()
    return started


def own_columns(ref, t):
    odd = lax.rem(t, 2)
    start = pl.multiple_of(t * COLS - odd * 64, 128)
    window = ref[:, pl.ds(start, WIDE)]
    return jnp.where(odd == 1, window[:, 64:WIDE], window[:, 0:COLS])


def prepare(
    qd_hbm, pu_hbm, states_hbm, kvw_hbm, gain_hbm, out, x_out, xt_out, st_out,
    qd, pu, states, kvw, gain, act, part, sems,
):
    waits = copies(
        [
            (states_hbm, states),
            (gain_hbm, gain),
            (kvw_hbm, kvw),
            (qd_hbm, qd),
            (pu_hbm, pu),
        ],
        sems,
    )
    t = lax.axis_index("tensor")
    waits[0].wait()
    for g in range(GAMES):
        act[4 * g : 4 * g + 4, :] = states[g].astype(f32)
    st_out[...] = own_columns(act, t)
    values = act[...]
    scale = lax.rsqrt(jnp.mean(values * values, axis=-1, keepdims=True) + epsilon)
    waits[1].wait()
    gains = gain[...].astype(f32)
    for c in range(D // 128):
        lanes = slice(128 * c, 128 * c + 128)
        x = (values[:, lanes] * scale * gains[c : c + 1, :]).astype(bf16)
        x_out[:, lanes] = x
        act[:, lanes] = x.astype(f32)
    xt = own_columns(act, t)
    xt_out[...] = xt
    waits[2].wait()
    for n in range(2):
        part[:, 512 * n : 512 * n + 512] = dot(xt.astype(bf16), kvw[n])
    for copy in waits[3:]:
        copy.wait()
    shared = jnp.concatenate([qd[...], pu[0], pu[1]], axis=1)
    for d in range(N):
        k, g = d // 4, d % 4
        rows = slice(4 * g, 4 * g + 4)
        out[d, 0:4, :] = shared
        out[d, 4:8, 0:128] = part[rows, 128 * k : 128 * k + 128]
        out[d, 4:8, 128:256] = part[rows, 512 + 128 * k : 640 + 128 * k]
        out[d, 4:8, 256:384] = jnp.zeros((4, 128), f32)


def regroup(recv, own, out, base_out, line):
    t = lax.axis_index("tensor")
    base = recv[0]
    for s in range(1, N):
        base += recv[s]
    base_out[...] = base
    for p in range(N // 2):
        line[:, 640 * p : 640 * p + 640] = jnp.concatenate(
            [recv[2 * p, 0:4, 0:COLS], recv[2 * p + 1, 0:4, 0:COLS]], axis=1
        )
    line[:, D : D + 1536] = own[...]
    pairs = [recv[4 * (t // 4) + c, 0:4, COLS:WIDE] for c in range(4)]
    line[:, D + 1536 : FULL] = jnp.concatenate(
        [c[:, 32 * n : 32 * n + 32] for n in range(2) for c in pairs], axis=1
    )
    for d in range(N):
        out[d] = line[:, HALF * (d % 2) : HALF * (d % 2) + HALF]


def assemble(recv, out):
    for c in range(2):
        for g in range(N):
            out[c, 4 * g : 4 * g + 4, :] = recv[g]


def columns(recv, start, width):
    if start + width <= HALF:
        return recv[0, :, start : start + width]
    if start >= HALF:
        return recv[1, :, start - HALF : start - HALF + width]
    left = recv[0, :, start:HALF]
    return jnp.concatenate([left, recv[1, :, 0 : start + width - HALF]], axis=1)


def rotate(values, cosine, sine):
    return values * cosine + pltpu.roll(values, HD // 2, 1) * sine


def head_norm(values, gain):
    return values * lax.rsqrt(jnp.mean(values * values, axis=-1, keepdims=True) + epsilon) * gain


def split(values):
    high = values.astype(bf16)
    rest = values - high.astype(f32)
    middle = rest.astype(bf16)
    return high, middle, (rest - middle.astype(f32)).astype(bf16)


def merge_queries(recv, qwt, x, xt, gains, cos, sin, out, od_out, ou_out, up_out):
    od_out[...] = columns(recv, 6016, 256)
    ou_out[...] = columns(recv, 6272, COLS)
    for n in range(2):
        up_out[n] = columns(recv, 6656 + 128 * n, 128)
    uh, um, ul = [u.astype(f32) for u in split(columns(recv, 5760, 256))]
    ups = jnp.concatenate([uh, uh, um, um, ul, uh], axis=0).T.astype(bf16)
    raw = jnp.zeros((ROWS, 256), f32)
    for p in range(N // 2):
        lanes = slice(640 * p, 640 * p + 640)
        h, m, l = split(columns(recv, 640 * p, 640))
        update = dot(ups, jnp.concatenate([h, m, h, m, h, l], axis=0))
        merged = (qwt[:, lanes].astype(f32) + 2.0 * update).astype(bf16)
        raw += dot(x[:, lanes], merged, ((1,), (1,)))
    cosine = jnp.concatenate([cos[g] for g in range(GAMES)], axis=0)
    sine = jnp.concatenate([sin[g] for g in range(GAMES)], axis=0)
    heads = []
    for h in range(2):
        v = head_norm(raw[:, HD * h : HD * h + HD], gains[0:1, :])
        heads.append(rotate(v, cosine, sine))
    low = [dot(xt[...], columns(recv, D + COLS * n, COLS), ((1,), (1,)), HIGHEST) for n in range(2)]
    low = [part.astype(f32) for part in split(jnp.concatenate(low, axis=1))]
    rows = [slice(4 * g, 4 * g + 4) for g in range(GAMES)]
    queries = [heads[j][r] for r in rows for j in range(2)]
    for d in range(N):
        own = rows[d % 4]
        piece = queries + [part[own] for part in low] + [jnp.zeros((4, HD), f32)]
        out[d] = jnp.concatenate(piece, axis=0).astype(bf16)


def fresh_pair(recv, base, up, gains, cos4, sin4, t):
    total = recv[0, 32:48, :].astype(f32)
    for s in range(1, N):
        total += recv[s, 32:48, :].astype(f32)
    low = total[0:4] + total[4:8] + total[8:12]
    low = jnp.concatenate([low, jnp.zeros((4, 128), f32)], axis=0)
    sums = jnp.concatenate([base[4:8, :], jnp.zeros((4, WIDE), f32)], axis=0)
    keys = sums[:, 0:128] + 2.0 * dot(low[:, 0:64], up[0], precision=HIGHEST)
    values = sums[:, 128:256] + 2.0 * dot(low[:, 64:128], up[1], precision=HIGHEST)
    game = lax.rem(t, 4)
    zeros = jnp.zeros((4, HD), f32)
    cosine = jnp.concatenate([cos4[game], zeros], axis=0)
    sine = jnp.concatenate([sin4[game], zeros], axis=0)
    keys = rotate(head_norm(keys, gains[1:2, :]), cosine, sine)
    return keys, values


def softmax(scores, valid):
    scores = jnp.where(valid, scores * score_scale, masked_score)
    peak = jnp.max(scores, axis=-1, keepdims=True)
    weights = jnp.where(valid, jnp.exp(scores - peak), 0.0)
    return peak, jnp.sum(weights, axis=-1, keepdims=True), weights.astype(bf16)


def as_row(column, eye):
    return jnp.sum(jnp.where(eye, column, 0.0), axis=0, keepdims=True)


def attend(lengths, recv, ck, cv, base, up, gains, cos4, sin4, out, qs, ms, ls, accs):
    t = lax.axis_index("tensor")
    fk, fv = fresh_pair(recv, base, up, gains, cos4, sin4, t)
    slot = t * BLOCK + lax.broadcasted_iota(jnp.int32, (1, BLOCK), 1)
    pairs = [(k, g) for k in range(KVH) for g in range(GAMES)]
    lanes = [slice(HD * k, HD * k + HD) for k in range(KVH)]
    wide = [recv[s, 0:32, :].astype(f32) for s in range(N)]
    scores = []
    for k, g in pairs:
        rows = slice(8 * g, 8 * g + 8)
        q = jnp.concatenate([w[rows] for w in wide[4 * k : 4 * k + 4]], axis=0).astype(bf16)
        qs[4 * k + g] = q
        scores.append(dot(q, ck[g, :, lanes[k]], ((1,), (1,))))
    valid = [jnp.broadcast_to(slot < lengths[g], (32, BLOCK)) for g in range(GAMES)]
    valid = jnp.concatenate(valid * KVH, axis=0)
    peak, total, weights = softmax(jnp.concatenate(scores, axis=0), valid)
    for n, (k, g) in enumerate(pairs):
        rows = slice(32 * n, 32 * n + 32)
        ms[n] = peak[rows]
        ls[n] = total[rows]
        accs[n] = dot(weights[rows], cv[g, :, lanes[k]])
    zeros = jnp.zeros((120, HD), f32)
    keys = jnp.concatenate([fk, zeros], axis=0).astype(bf16)
    values = jnp.concatenate([fv, zeros], axis=0).astype(bf16)
    step = lax.rem(lax.broadcasted_iota(jnp.int32, (32, HD), 0), 4)
    causal = lax.broadcasted_iota(jnp.int32, (32, HD), 1) <= step
    fresh_peak, fresh_sum, fresh_weights = softmax(dot(qs[t], keys, ((1,), (1,))), causal)
    fresh_acc = dot(fresh_weights, values)
    highest = jnp.maximum(ms[t], fresh_peak)
    old, new = jnp.exp(ms[t] - highest), jnp.exp(fresh_peak - highest)
    ls[t] = ls[t] * old + fresh_sum * new
    accs[t] = accs[t] * old + fresh_acc * new
    ms[t] = highest
    ones = [lax.broadcasted_iota(jnp.int32, (128, 128), n) for n in range(2)]
    eye = ones[0] == ones[1]
    order = [(i, g) for i in range(4) for g in range(GAMES)]
    for k in range(KVH):
        stats = []
        for ref in (ms, ls):
            column = [ref[4 * k + g, 8 * i : 8 * i + 8, :] for i, g in order]
            row = as_row(jnp.concatenate(column, axis=0), eye)
            stats += [part.astype(f32) for part in split(row)]
        stats = jnp.concatenate(stats + [jnp.zeros((2, 128), f32)], axis=0)
        for i in range(4):
            mine = [accs[4 * k + g, 8 * i : 8 * i + 8, :] for g in range(GAMES)]
            own = pltpu.roll(stats, 128 - 32 * i, 1) if i else stats
            piece = jnp.concatenate(mine + [own, jnp.zeros((8, 128), f32)], axis=0)
            out[4 * k + i] = piece.astype(bf16)


def project(recv, ow, od, out):
    tails = [recv[s, 32:48, :].astype(f32) for s in range(N)]
    peaks = jnp.concatenate([p[0:1] + p[1:2] + p[2:3] for p in tails], axis=0)
    sums = jnp.concatenate([p[3:4] + p[4:5] + p[5:6] for p in tails], axis=0)
    highest = jnp.max(peaks, axis=0, keepdims=True)
    scale = jnp.exp(peaks - highest)
    total = jnp.sum(sums * scale, axis=0, keepdims=True)
    share = scale / total
    share = jnp.concatenate([share, jnp.zeros((112, 128), f32)], axis=0).T
    acc = jnp.zeros((32, HD), f32)
    for s in range(N):
        acc += recv[s, 0:32, :].astype(f32) * share[0:32, s : s + 1]
    halves = [
        jnp.concatenate([acc[8 * g + 4 * j : 8 * g + 4 * j + 4] for g in range(GAMES)], axis=0)
        for j in range(2)
    ]
    attended = jnp.concatenate(halves, axis=1).astype(bf16)
    low = dot(attended.astype(f32), od[...], ((1,), (1,)), HIGHEST)
    for p in range(N // 2):
        part = dot(attended, ow[:, 640 * p : 640 * p + 640])
        out[2 * p] = jnp.concatenate([part[:, 0:COLS], low], axis=1).astype(bf16)
        out[2 * p + 1] = jnp.concatenate([part[:, COLS:640], low], axis=1).astype(bf16)


def add_residual(recv, ou, st, out):
    total = recv[0].astype(f32)
    for s in range(1, N):
        total += recv[s].astype(f32)
    projected = total[:, 0:COLS] + 2.0 * dot(total[:, COLS:WIDE], ou[...], precision=HIGHEST)
    stream = st[...] + projected
    squares = jnp.sum(stream * stream, axis=-1, keepdims=True)
    high = squares.astype(bf16).astype(f32)
    middle = (squares - high).astype(bf16).astype(f32)
    low = squares - high - middle
    lane = lax.broadcasted_iota(jnp.int32, (ROWS, RANK), 1)
    tail = jnp.where(lane == 0, high, 0.0)
    tail = jnp.where(lane == 1, middle, tail)
    tail = jnp.where(lane == 2, low, tail)
    piece = jnp.concatenate([stream, tail], axis=1).astype(bf16)
    for d in range(N):
        out[d] = piece


def finish(recv, gain, residual, normed):
    squares = jnp.zeros((ROWS, RANK), f32)
    for s in range(N):
        squares += recv[s, :, COLS:WIDE].astype(f32)
    mean = jnp.sum(squares, axis=-1, keepdims=True) * (1.0 / D)
    scale = lax.rsqrt(mean + epsilon)
    gains = gain[...].astype(f32)
    for p in range(N // 2):
        lanes = slice(640 * p, 640 * p + 640)
        both = jnp.concatenate(
            [recv[2 * p, :, 0:COLS].astype(f32), recv[2 * p + 1, :, 0:COLS].astype(f32)], axis=1
        )
        own = jnp.concatenate([gains[5 * p + c : 5 * p + c + 1, :] for c in range(5)], axis=1)
        scaled = both * scale * own
        for g in range(GAMES):
            rows = slice(4 * g, 4 * g + 4)
            residual[g, :, lanes] = both[rows].astype(bf16)
            normed[g, :, lanes] = scaled[rows].astype(bf16)


def exchange(array, axis):
    return lax.all_to_all(array, axis, 0, 0, tiled=True)


def rope_tables(lengths):
    positions = lengths[:, None] + jnp.arange(STEPS, dtype=jnp.int32)[None, :]
    inverse = rope_theta ** (-(jnp.arange(HD // 2, dtype=f32) * 2.0 / HD))
    angles = positions.astype(f32)[..., None] * inverse
    cos, sin = jnp.cos(angles), jnp.sin(angles)
    return jnp.concatenate([cos, cos], axis=-1), jnp.concatenate([-sin, sin], axis=-1)


def local(
    states,
    input_gain,
    post_gain,
    norm_gains,
    query_weight,
    key_value_weight,
    output_weight,
    query_down,
    query_up,
    pair_down,
    pair_up,
    output_down,
    output_up,
    cache_keys,
    cache_values,
    lengths,
):
    shape = jax.ShapeDtypeStruct
    cos, sin = rope_tables(lengths)
    dma = pltpu.SemaphoreType.DMA
    shared, x, own_x, own_states = run(
        prepare,
        (
            shape((N, 8, WIDE), f32),
            shape((ROWS, D), bf16),
            shape((ROWS, COLS), f32),
            shape((ROWS, COLS), f32),
        ),
        (
            query_down.T,
            pair_up,
            states,
            key_value_weight,
            input_gain.reshape(D // 128, 128),
        ),
        "prepare",
        specs=[HBM] * 5,
        limit=60 << 20,
        scratch=[
            pltpu.VMEM((4, COLS), f32),
            pltpu.VMEM((2, 4, 32), f32),
            pltpu.VMEM((GAMES, STEPS, D), bf16),
            pltpu.VMEM((2, COLS, 512), bf16),
            pltpu.VMEM((D // 128, 128), bf16),
            pltpu.VMEM((ROWS, D), f32),
            pltpu.VMEM((ROWS, 1024), f32),
            dma((5,)),
        ],
    )
    own = jnp.concatenate(
        [
            pair_down[0].T,
            pair_down[1].T,
            query_up,
            output_down.T,
            output_up,
            jnp.zeros((4, 64), f32),
        ],
        axis=1,
    )
    shared, own, cos, sin, query_turned = lax.optimization_barrier(
        (exchange(shared, "tensor"), own, cos, sin, query_weight.T)
    )
    factors, base = run(
        regroup,
        (shape((N, 4, HALF), f32), shape((8, WIDE), f32)),
        (shared, own),
        "regroup",
        scratch=[pltpu.VMEM((4, FULL), f32)],
    )
    factors = exchange(factors, "group")
    factors = run(assemble, shape((2, RANK, HALF), f32), (factors,), "assemble")
    pairs = [[2 * i, 2 * i + 1] for i in range(N // 2)]
    factors = lax.all_to_all(factors, "group", 0, 0, tiled=True, axis_index_groups=pairs)
    queries, down_output, up_output, up_pair = run(
        merge_queries,
        (
            shape((N, 48, HD), bf16),
            shape((RANK, 256), f32),
            shape((RANK, COLS), f32),
            shape((2, RANK, HD), f32),
        ),
        (factors, query_turned, x, own_x, norm_gains, cos, sin),
        "merge_queries",
    )
    queries = exchange(queries, "tensor")
    partials = run(
        attend,
        shape((N, 48, HD), bf16),
        (
            lengths,
            queries,
            cache_keys,
            cache_values,
            base,
            up_pair,
            norm_gains,
            cos,
            sin,
        ),
        "attend",
        specs=[SMEM] + [VMEM] * 8,
        scratch=[
            pltpu.VMEM((N, 32, HD), bf16),
            pltpu.VMEM((N, 32, 1), f32),
            pltpu.VMEM((N, 32, 1), f32),
            pltpu.VMEM((N, 32, HD), f32),
        ],
    )
    partials = exchange(partials, "tensor")
    projected = run(
        project, shape((N, ROWS, WIDE), bf16), (partials, output_weight, down_output), "project"
    )
    projected = exchange(projected, "tensor")
    pieces = run(
        add_residual,
        shape((N, ROWS, WIDE), bf16),
        (projected, up_output, own_states),
        "add_residual",
    )
    pieces = exchange(pieces, "tensor")
    return run(
        finish,
        (shape((GAMES, STEPS, D), bf16), shape((GAMES, STEPS, D), bf16)),
        (pieces, post_gain.reshape(D // 128, 128)),
        "finish",
    )


def solution(mesh):
    in_specs = (
        P("group", None, None),
        P(),
        P(),
        P(),
        P(None, "tensor"),
        P(None, "tensor", None),
        P("tensor", None),
        P("tensor", "group"),
        P("group", "tensor"),
        P(None, "tensor", "group"),
        P(None, "group", "tensor"),
        P("tensor", "group"),
        P("group", "tensor"),
        P("group", "tensor", None),
        P("group", "tensor", None),
        P("group"),
    )
    out_specs = (P("group", None, None), P("group", None, None))
    return jax.shard_map(local, mesh=mesh, in_specs=in_specs, out_specs=out_specs, check_vma=False)
```

```python
import functools
import math

import jax
import jax.numpy as jnp
from jax import lax
from jax.experimental import pallas as pl
from jax.experimental.pallas import tpu as pltpu
from jax.sharding import PartitionSpec as P

HD = 128
QH = 32
KVH = 4
N = 16
ROWS = 16
GAMES = 4
STEPS = 4
RANK = 64
D = 5120
COLS = D // N
WIDE = COLS + RANK
BLOCK = 256
FULL = D + 1792
HALF = FULL // 2

epsilon = 1e-06
rope_theta = 1000000.0
masked_score = -1e30
score_scale = 1.0 / math.sqrt(HD)
HIGHEST = lax.Precision.HIGHEST
f32 = jnp.float32
bf16 = jnp.bfloat16

VMEM = pl.BlockSpec(memory_space=pltpu.VMEM)
SMEM = pl.BlockSpec(memory_space=pltpu.SMEM)
HBM = pl.BlockSpec(memory_space=pltpu.HBM)


def dot(a, b, contract=((1,), (0,)), precision=None):
    return lax.dot_general(
        a, b, (contract, ((), ())), precision=precision, preferred_element_type=f32
    )


def run(body, outs, args, name, specs=None, scratch=(), limit=48 << 20):
    return pl.pallas_call(
        body,
        out_shape=outs,
        in_specs=specs or [VMEM] * len(args),
        out_specs=jax.tree.map(lambda _: VMEM, outs),
        scratch_shapes=list(scratch),
        compiler_params=pltpu.CompilerParams(vmem_limit_bytes=limit),
        name=name,
    )(*args)


def copies(pairs, sems):
    started = [pltpu.make_async_copy(src, dst, sems.at[i]) for i, (src, dst) in enumerate(pairs)]
    for copy in started:
        copy.start()
    return started


def own_columns(ref, t):
    odd = lax.rem(t, 2)
    start = pl.multiple_of(t * COLS - odd * 64, 128)
    window = ref[:, pl.ds(start, WIDE)]
    return jnp.where(odd == 1, window[:, 64:WIDE], window[:, 0:COLS])


def prepare(
    qd_hbm, pu_hbm, states_hbm, kvw_hbm, gain_hbm, out, x_out, xt_out, st_out,
    qd, pu, states, kvw, gain, act, part, sems,
):
    waits = copies(
        [
            (states_hbm, states),
            (gain_hbm, gain),
            (kvw_hbm, kvw),
            (qd_hbm, qd),
            (pu_hbm, pu),
        ],
        sems,
    )
    t = lax.axis_index("tensor")
    waits[0].wait()
    for g in range(GAMES):
        act[4 * g : 4 * g + 4, :] = states[g].astype(f32)
    st_out[...] = own_columns(act, t)
    values = act[...]
    scale = lax.rsqrt(jnp.mean(values * values, axis=-1, keepdims=True) + epsilon)
    waits[1].wait()
    gains = gain[...].astype(f32)
    for c in range(D // 128):
        lanes = slice(128 * c, 128 * c + 128)
        x = (values[:, lanes] * scale * gains[c : c + 1, :]).astype(bf16)
        x_out[:, lanes] = x
        act[:, lanes] = x.astype(f32)
    xt = own_columns(act, t)
    xt_out[...] = xt
    waits[2].wait()
    for n in range(2):
        part[:, 512 * n : 512 * n + 512] = dot(xt.astype(bf16), kvw[n])
    for copy in waits[3:]:
        copy.wait()
    shared = jnp.concatenate([qd[...], pu[0], pu[1]], axis=1)
    for d in range(N):
        k, g = d // 4, d % 4
        rows = slice(4 * g, 4 * g + 4)
        out[d, :, 0:WIDE] = shared
        out[d, :, WIDE : WIDE + 128] = part[rows, 128 * k : 128 * k + 128]
        out[d, :, WIDE + 128 : 640] = part[rows, 512 + 128 * k : 640 + 128 * k]


def regroup(recv, own, out, base_out, line):
    t = lax.axis_index("tensor")
    base = recv[0, :, WIDE:640]
    for s in range(1, N):
        base += recv[s, :, WIDE:640]
    base_out[...] = base
    for p in range(N // 2):
        line[:, 640 * p : 640 * p + 640] = jnp.concatenate(
            [recv[2 * p, 0:4, 0:COLS], recv[2 * p + 1, 0:4, 0:COLS]], axis=1
        )
    line[:, D : D + 1536] = own[...]
    pairs = [recv[4 * (t // 4) + c, 0:4, COLS:WIDE] for c in range(4)]
    line[:, D + 1536 : FULL] = jnp.concatenate(
        [c[:, 32 * n : 32 * n + 32] for n in range(2) for c in pairs], axis=1
    )
    for d in range(N):
        out[d] = line[:, HALF * (d % 2) : HALF * (d % 2) + HALF]


def assemble(recv, out):
    for c in range(2):
        for g in range(N):
            out[c, 4 * g : 4 * g + 4, :] = recv[g]


def columns(recv, start, width):
    if start + width <= HALF:
        return recv[0, :, start : start + width]
    if start >= HALF:
        return recv[1, :, start - HALF : start - HALF + width]
    left = recv[0, :, start:HALF]
    return jnp.concatenate([left, recv[1, :, 0 : start + width - HALF]], axis=1)


def rotate(values, cosine, sine):
    return values * cosine + pltpu.roll(values, HD // 2, 1) * sine


def head_norm(values, gain):
    return values * lax.rsqrt(jnp.mean(values * values, axis=-1, keepdims=True) + epsilon) * gain


def split(values):
    high = values.astype(bf16)
    rest = values - high.astype(f32)
    middle = rest.astype(bf16)
    return high, middle, (rest - middle.astype(f32)).astype(bf16)


def merge_queries(recv, qwt, x, xt, gains, cos, sin, out, od_out, ou_out, up_out):
    od_out[...] = columns(recv, 6016, 256)
    ou_out[...] = columns(recv, 6272, COLS)
    for n in range(2):
        up_out[n] = columns(recv, 6656 + 128 * n, 128)
    uh, um, ul = [u.astype(f32) for u in split(columns(recv, 5760, 256))]
    ups = jnp.concatenate([uh, uh, um, um, ul, uh], axis=0).T.astype(bf16)
    raw = jnp.zeros((ROWS, 256), f32)
    for p in range(N // 2):
        lanes = slice(640 * p, 640 * p + 640)
        h, m, l = split(columns(recv, 640 * p, 640))
        update = dot(ups, jnp.concatenate([h, m, h, m, h, l], axis=0))
        merged = (qwt[:, lanes].astype(f32) + 2.0 * update).astype(bf16)
        raw += dot(x[:, lanes], merged, ((1,), (1,)))
    cosine = jnp.concatenate([cos[g] for g in range(GAMES)], axis=0)
    sine = jnp.concatenate([sin[g] for g in range(GAMES)], axis=0)
    heads = []
    for h in range(2):
        v = head_norm(raw[:, HD * h : HD * h + HD], gains[0:1, :])
        heads.append(rotate(v, cosine, sine))
    low = [dot(xt[...], columns(recv, D + COLS * n, COLS), ((1,), (1,)), HIGHEST) for n in range(2)]
    low = [part.astype(f32) for part in split(jnp.concatenate(low, axis=1))[0:2]]
    rows = [slice(4 * g, 4 * g + 4) for g in range(GAMES)]
    queries = [heads[j][r] for r in rows for j in range(2)]
    for d in range(N):
        own = rows[d % 4]
        piece = queries + [part[own] for part in low]
        out[d] = jnp.concatenate(piece, axis=0).astype(bf16)


def fresh_pair(recv, base, up, gains, cos4, sin4, t):
    total = recv[0, 32:40, :].astype(f32)
    for s in range(1, N):
        total += recv[s, 32:40, :].astype(f32)
    low = total[0:4] + total[4:8]
    low = jnp.concatenate([low, jnp.zeros((4, 128), f32)], axis=0)
    sums = jnp.concatenate([base[...], jnp.zeros((4, 256), f32)], axis=0)
    keys = sums[:, 0:128] + 2.0 * dot(low[:, 0:64], up[0], precision=HIGHEST)
    values = sums[:, 128:256] + 2.0 * dot(low[:, 64:128], up[1], precision=HIGHEST)
    game = lax.rem(t, 4)
    zeros = jnp.zeros((4, HD), f32)
    cosine = jnp.concatenate([cos4[game], zeros], axis=0)
    sine = jnp.concatenate([sin4[game], zeros], axis=0)
    keys = rotate(head_norm(keys, gains[1:2, :]), cosine, sine)
    return keys, values


def softmax(scores, valid):
    scores = jnp.where(valid, scores * score_scale, masked_score)
    peak = jnp.max(scores, axis=-1, keepdims=True)
    weights = jnp.where(valid, jnp.exp(scores - peak), 0.0)
    return peak, jnp.sum(weights, axis=-1, keepdims=True), weights.astype(bf16)


def as_row(column, eye):
    return jnp.sum(jnp.where(eye, column, 0.0), axis=0, keepdims=True)


def attend(lengths, recv, ck, cv, base, up, gains, cos4, sin4, out, qs, ms, ls, accs):
    t = lax.axis_index("tensor")
    fk, fv = fresh_pair(recv, base, up, gains, cos4, sin4, t)
    slot = t * BLOCK + lax.broadcasted_iota(jnp.int32, (1, BLOCK), 1)
    pairs = [(k, g) for k in range(KVH) for g in range(GAMES)]
    lanes = [slice(HD * k, HD * k + HD) for k in range(KVH)]
    wide = [recv[s, 0:32, :].astype(f32) for s in range(N)]
    scores = []
    for k, g in pairs:
        rows = slice(8 * g, 8 * g + 8)
        q = jnp.concatenate([w[rows] for w in wide[4 * k : 4 * k + 4]], axis=0).astype(bf16)
        qs[4 * k + g] = q
        scores.append(dot(q, ck[g, :, lanes[k]], ((1,), (1,))))
    valid = [jnp.broadcast_to(slot < lengths[g], (32, BLOCK)) for g in range(GAMES)]
    valid = jnp.concatenate(valid * KVH, axis=0)
    peak, total, weights = softmax(jnp.concatenate(scores, axis=0), valid)
    for n, (k, g) in enumerate(pairs):
        rows = slice(32 * n, 32 * n + 32)
        ms[n] = peak[rows]
        ls[n] = total[rows]
        accs[n] = dot(weights[rows], cv[g, :, lanes[k]])
    zeros = jnp.zeros((120, HD), f32)
    keys = jnp.concatenate([fk, zeros], axis=0).astype(bf16)
    values = jnp.concatenate([fv, zeros], axis=0).astype(bf16)
    step = lax.rem(lax.broadcasted_iota(jnp.int32, (32, HD), 0), 4)
    causal = lax.broadcasted_iota(jnp.int32, (32, HD), 1) <= step
    fresh_peak, fresh_sum, fresh_weights = softmax(dot(qs[t], keys, ((1,), (1,))), causal)
    fresh_acc = dot(fresh_weights, values)
    highest = jnp.maximum(ms[t], fresh_peak)
    old, new = jnp.exp(ms[t] - highest), jnp.exp(fresh_peak - highest)
    ls[t] = ls[t] * old + fresh_sum * new
    accs[t] = accs[t] * old + fresh_acc * new
    ms[t] = highest
    ones = [lax.broadcasted_iota(jnp.int32, (128, 128), n) for n in range(2)]
    eye = ones[0] == ones[1]
    order = [(i, g) for i in range(4) for g in range(GAMES)]
    for k in range(KVH):
        stats = []
        for ref in (ms, ls):
            column = [ref[4 * k + g, 8 * i : 8 * i + 8, :] for i, g in order]
            row = as_row(jnp.concatenate(column, axis=0), eye)
            stats += [part.astype(f32) for part in split(row)]
        stats = jnp.concatenate(stats + [jnp.zeros((2, 128), f32)], axis=0)
        for i in range(4):
            mine = [accs[4 * k + g, 8 * i : 8 * i + 8, :] for g in range(GAMES)]
            own = pltpu.roll(stats, 128 - 32 * i, 1) if i else stats
            piece = jnp.concatenate(mine + [own], axis=0)
            out[4 * k + i] = piece.astype(bf16)


def project(recv, ow, od, out):
    tails = [recv[s, 32:40, :].astype(f32) for s in range(N)]
    peaks = jnp.concatenate([p[0:1] + p[1:2] + p[2:3] for p in tails], axis=0)
    sums = jnp.concatenate([p[3:4] + p[4:5] + p[5:6] for p in tails], axis=0)
    highest = jnp.max(peaks, axis=0, keepdims=True)
    scale = jnp.exp(peaks - highest)
    total = jnp.sum(sums * scale, axis=0, keepdims=True)
    share = scale / total
    share = jnp.concatenate([share, jnp.zeros((112, 128), f32)], axis=0).T
    acc = jnp.zeros((32, HD), f32)
    for s in range(N):
        acc += recv[s, 0:32, :].astype(f32) * share[0:32, s : s + 1]
    halves = [
        jnp.concatenate([acc[8 * g + 4 * j : 8 * g + 4 * j + 4] for g in range(GAMES)], axis=0)
        for j in range(2)
    ]
    attended = jnp.concatenate(halves, axis=1).astype(bf16)
    low = dot(attended.astype(f32), od[...], ((1,), (1,)), HIGHEST)
    for p in range(N // 2):
        part = dot(attended, ow[:, 640 * p : 640 * p + 640])
        out[2 * p] = jnp.concatenate([part[:, 0:COLS], low], axis=1).astype(bf16)
        out[2 * p + 1] = jnp.concatenate([part[:, COLS:640], low], axis=1).astype(bf16)


def add_residual(recv, ou, st, out):
    total = recv[0].astype(f32)
    for s in range(1, N):
        total += recv[s].astype(f32)
    projected = total[:, 0:COLS] + 2.0 * dot(total[:, COLS:WIDE], ou[...], precision=HIGHEST)
    stream = st[...] + projected
    tail = jnp.concatenate([stream[0:8, 256:COLS], stream[8:16, 256:COLS]], axis=1)
    piece = jnp.concatenate([stream[:, 0:128], stream[:, 128:256], tail], axis=0).astype(bf16)
    for d in range(N):
        out[d] = piece


def finish(recv, gain, residual, normed, stream):
    squares = jnp.zeros((ROWS, 128), f32)
    for p in range(N // 2):
        parts = []
        for s in (2 * p, 2 * p + 1):
            whole = recv[s].astype(f32)
            tail = whole[32:40]
            parts += [whole[0:16], whole[16:32]]
            parts.append(jnp.concatenate([tail[:, 0:64], tail[:, 64:128]], axis=0))
        both = jnp.concatenate(parts, axis=1)
        stream[:, 640 * p : 640 * p + 640] = both
        for c in range(5):
            squares += both[:, 128 * c : 128 * c + 128] ** 2
    mean = jnp.sum(squares, axis=-1, keepdims=True) * (1.0 / D)
    scale = lax.rsqrt(mean + epsilon)
    gains = gain[...].astype(f32)
    for p in range(N // 2):
        lanes = slice(640 * p, 640 * p + 640)
        both = stream[:, lanes]
        own = jnp.concatenate([gains[5 * p + c : 5 * p + c + 1, :] for c in range(5)], axis=1)
        scaled = both * scale * own
        for g in range(GAMES):
            rows = slice(4 * g, 4 * g + 4)
            residual[g, :, lanes] = both[rows].astype(bf16)
            normed[g, :, lanes] = scaled[rows].astype(bf16)


def exchange(array, axis):
    return lax.all_to_all(array, axis, 0, 0, tiled=True)


def rope_tables(lengths):
    positions = lengths[:, None] + jnp.arange(STEPS, dtype=jnp.int32)[None, :]
    inverse = rope_theta ** (-(jnp.arange(HD // 2, dtype=f32) * 2.0 / HD))
    angles = positions.astype(f32)[..., None] * inverse
    cos, sin = jnp.cos(angles), jnp.sin(angles)
    return jnp.concatenate([cos, cos], axis=-1), jnp.concatenate([-sin, sin], axis=-1)


def local(
    states,
    input_gain,
    post_gain,
    norm_gains,
    query_weight,
    key_value_weight,
    output_weight,
    query_down,
    query_up,
    pair_down,
    pair_up,
    output_down,
    output_up,
    cache_keys,
    cache_values,
    lengths,
):
    shape = jax.ShapeDtypeStruct
    cos, sin = rope_tables(lengths)
    dma = pltpu.SemaphoreType.DMA
    shared, x, own_x, own_states = run(
        prepare,
        (
            shape((N, 4, 640), f32),
            shape((ROWS, D), bf16),
            shape((ROWS, COLS), f32),
            shape((ROWS, COLS), f32),
        ),
        (
            query_down.T,
            pair_up,
            states,
            key_value_weight,
            input_gain.reshape(D // 128, 128),
        ),
        "prepare",
        specs=[HBM] * 5,
        limit=60 << 20,
        scratch=[
            pltpu.VMEM((4, COLS), f32),
            pltpu.VMEM((2, 4, 32), f32),
            pltpu.VMEM((GAMES, STEPS, D), bf16),
            pltpu.VMEM((2, COLS, 512), bf16),
            pltpu.VMEM((D // 128, 128), bf16),
            pltpu.VMEM((ROWS, D), f32),
            pltpu.VMEM((ROWS, 1024), f32),
            dma((5,)),
        ],
    )
    own = jnp.concatenate(
        [
            pair_down[0].T,
            pair_down[1].T,
            query_up,
            output_down.T,
            output_up,
            jnp.zeros((4, 64), f32),
        ],
        axis=1,
    )
    shared, own, cos, sin, query_turned = lax.optimization_barrier(
        (exchange(shared, "tensor"), own, cos, sin, query_weight.T)
    )
    factors, base = run(
        regroup,
        (shape((N, 4, HALF), f32), shape((4, 256), f32)),
        (shared, own),
        "regroup",
        scratch=[pltpu.VMEM((4, FULL), f32)],
    )
    factors = exchange(factors, "group")
    factors = run(assemble, shape((2, RANK, HALF), f32), (factors,), "assemble")
    pairs = [[2 * i, 2 * i + 1] for i in range(N // 2)]
    factors = lax.all_to_all(factors, "group", 0, 0, tiled=True, axis_index_groups=pairs)
    queries, down_output, up_output, up_pair = run(
        merge_queries,
        (
            shape((N, 40, HD), bf16),
            shape((RANK, 256), f32),
            shape((RANK, COLS), f32),
            shape((2, RANK, HD), f32),
        ),
        (factors, query_turned, x, own_x, norm_gains, cos, sin),
        "merge_queries",
    )
    queries = exchange(queries, "tensor")
    partials = run(
        attend,
        shape((N, 40, HD), bf16),
        (
            lengths,
            queries,
            cache_keys,
            cache_values,
            base,
            up_pair,
            norm_gains,
            cos,
            sin,
        ),
        "attend",
        specs=[SMEM] + [VMEM] * 8,
        scratch=[
            pltpu.VMEM((N, 32, HD), bf16),
            pltpu.VMEM((N, 32, 1), f32),
            pltpu.VMEM((N, 32, 1), f32),
            pltpu.VMEM((N, 32, HD), f32),
        ],
    )
    partials = exchange(partials, "tensor")
    projected = run(
        project, shape((N, ROWS, WIDE), bf16), (partials, output_weight, down_output), "project"
    )
    projected = exchange(projected, "tensor")
    pieces = run(
        add_residual,
        shape((N, 40, HD), bf16),
        (projected, up_output, own_states),
        "add_residual",
    )
    pieces = exchange(pieces, "tensor")
    return run(
        finish,
        (shape((GAMES, STEPS, D), bf16), shape((GAMES, STEPS, D), bf16)),
        (pieces, post_gain.reshape(D // 128, 128)),
        "finish",
        scratch=[pltpu.VMEM((ROWS, D), f32)],
    )


def solution(mesh):
    in_specs = (
        P("group", None, None),
        P(),
        P(),
        P(),
        P(None, "tensor"),
        P(None, "tensor", None),
        P("tensor", None),
        P("tensor", "group"),
        P("group", "tensor"),
        P(None, "tensor", "group"),
        P(None, "group", "tensor"),
        P("tensor", "group"),
        P("group", "tensor"),
        P("group", "tensor", None),
        P("group", "tensor", None),
        P("group"),
    )
    out_specs = (P("group", None, None), P("group", None, None))
    return jax.shard_map(local, mesh=mesh, in_specs=in_specs, out_specs=out_specs, check_vma=False)
```

```python
import functools
import math

import jax
import jax.numpy as jnp
from jax import lax
from jax.experimental import pallas as pl
from jax.experimental.pallas import tpu as pltpu
from jax.sharding import PartitionSpec as P

HD = 128
QH = 32
KVH = 4
N = 16
ROWS = 16
GAMES = 4
STEPS = 4
RANK = 64
D = 5120
COLS = D // N
ORDER = list(range(0, N, 2)) + list(range(1, N, 2))
PLACE = [ORDER.index(t) for t in range(N)]
WIDE = COLS + RANK
BLOCK = 256
FULL = D + 1792
HALF = FULL // 2

epsilon = 1e-06
rope_theta = 1000000.0
masked_score = -1e30
score_scale = 1.0 / math.sqrt(HD)
HIGHEST = lax.Precision.HIGHEST
f32 = jnp.float32
bf16 = jnp.bfloat16

VMEM = pl.BlockSpec(memory_space=pltpu.VMEM)
SMEM = pl.BlockSpec(memory_space=pltpu.SMEM)
HBM = pl.BlockSpec(memory_space=pltpu.HBM)


def dot(a, b, contract=((1,), (0,)), precision=None):
    return lax.dot_general(
        a, b, (contract, ((), ())), precision=precision, preferred_element_type=f32
    )


def run(body, outs, args, name, specs=None, scratch=(), limit=48 << 20):
    return pl.pallas_call(
        body,
        out_shape=outs,
        in_specs=specs or [VMEM] * len(args),
        out_specs=jax.tree.map(lambda _: VMEM, outs),
        scratch_shapes=list(scratch),
        compiler_params=pltpu.CompilerParams(vmem_limit_bytes=limit),
        name=name,
    )(*args)


def copies(pairs, sems):
    started = [pltpu.make_async_copy(src, dst, sems.at[i]) for i, (src, dst) in enumerate(pairs)]
    for copy in started:
        copy.start()
    return started


def own_columns(ref, t):
    odd = lax.rem(t, 2)
    start = pl.multiple_of(t * COLS - odd * 64, 128)
    window = ref[:, pl.ds(start, WIDE)]
    return jnp.where(odd == 1, window[:, 64:WIDE], window[:, 0:COLS])


def prepare(
    qd_hbm, pu_hbm, states_hbm, kvw_hbm, gain_hbm, out, x_out, xt_out, st_out,
    qd, pu, states, kvw, gain, act, part, sems,
):
    waits = copies(
        [
            (states_hbm, states),
            (gain_hbm, gain),
            (kvw_hbm, kvw),
            (qd_hbm, qd),
            (pu_hbm, pu),
        ],
        sems,
    )
    t = lax.axis_index("tensor")
    waits[0].wait()
    for g in range(GAMES):
        act[4 * g : 4 * g + 4, :] = states[g].astype(f32)
    st_out[...] = own_columns(act, t)
    values = act[...]
    scale = lax.rsqrt(jnp.mean(values * values, axis=-1, keepdims=True) + epsilon)
    waits[1].wait()
    gains = gain[...].astype(f32)
    for c in range(D // 128):
        lanes = slice(128 * c, 128 * c + 128)
        x = (values[:, lanes] * scale * gains[c : c + 1, :]).astype(bf16)
        x_out[:, lanes] = x
        act[:, lanes] = x.astype(f32)
    xt = own_columns(act, t)
    xt_out[...] = xt
    waits[2].wait()
    for n in range(2):
        part[:, 512 * n : 512 * n + 512] = dot(xt.astype(bf16), kvw[n])
    for copy in waits[3:]:
        copy.wait()
    shared = jnp.concatenate([qd[...], pu[0], pu[1]], axis=1)
    for d in range(N):
        k, g = d // 4, d % 4
        rows = slice(4 * g, 4 * g + 4)
        out[PLACE[d], :, 0:WIDE] = shared
        out[PLACE[d], :, WIDE : WIDE + 128] = part[rows, 128 * k : 128 * k + 128]
        out[PLACE[d], :, WIDE + 128 : 640] = part[rows, 512 + 128 * k : 640 + 128 * k]


def regroup(recv, own, out, base_out, line):
    t = lax.axis_index("tensor")
    base = recv[0, :, WIDE:640]
    for s in range(1, N):
        base += recv[s, :, WIDE:640]
    base_out[...] = base
    for p in range(N // 2):
        line[:, 640 * p : 640 * p + 640] = jnp.concatenate(
            [recv[PLACE[2 * p + c], 0:4, 0:COLS] for c in range(2)], axis=1
        )
    line[:, D : D + 1536] = own[...]
    pairs = [recv[2 * (t // 4) + PLACE[c], 0:4, COLS:WIDE] for c in range(4)]
    line[:, D + 1536 : FULL] = jnp.concatenate(
        [c[:, 32 * n : 32 * n + 32] for n in range(2) for c in pairs], axis=1
    )
    for d in range(N):
        out[d] = line[:, HALF * (d % 2) : HALF * (d % 2) + HALF]


def assemble(recv, out):
    for c in range(2):
        for g in range(N):
            out[c, 4 * g : 4 * g + 4, :] = recv[g]


def columns(recv, start, width):
    if start + width <= HALF:
        return recv[0, :, start : start + width]
    if start >= HALF:
        return recv[1, :, start - HALF : start - HALF + width]
    left = recv[0, :, start:HALF]
    return jnp.concatenate([left, recv[1, :, 0 : start + width - HALF]], axis=1)


def rotate(values, cosine, sine):
    return values * cosine + pltpu.roll(values, HD // 2, 1) * sine


def head_norm(values, gain):
    return values * lax.rsqrt(jnp.mean(values * values, axis=-1, keepdims=True) + epsilon) * gain


def split(values):
    high = values.astype(bf16)
    rest = values - high.astype(f32)
    middle = rest.astype(bf16)
    return high, middle, (rest - middle.astype(f32)).astype(bf16)


def merge_queries(recv, qwt, x, xt, gains, cos, sin, out, od_out, ou_out, up_out):
    od_out[...] = columns(recv, 6016, 256)
    ou_out[...] = columns(recv, 6272, COLS)
    for n in range(2):
        up_out[n] = columns(recv, 6656 + 128 * n, 128)
    uh, um, ul = [u.astype(f32) for u in split(columns(recv, 5760, 256))]
    ups = jnp.concatenate([uh, uh, um, um, ul, uh], axis=0).T.astype(bf16)
    raw = jnp.zeros((ROWS, 256), f32)
    for p in range(N // 2):
        lanes = slice(640 * p, 640 * p + 640)
        h, m, l = split(columns(recv, 640 * p, 640))
        update = dot(ups, jnp.concatenate([h, m, h, m, h, l], axis=0))
        merged = (qwt[:, lanes].astype(f32) + 2.0 * update).astype(bf16)
        raw += dot(x[:, lanes], merged, ((1,), (1,)))
    cosine = jnp.concatenate([cos[g] for g in range(GAMES)], axis=0)
    sine = jnp.concatenate([sin[g] for g in range(GAMES)], axis=0)
    heads = []
    for h in range(2):
        v = head_norm(raw[:, HD * h : HD * h + HD], gains[0:1, :])
        heads.append(rotate(v, cosine, sine))
    low = [dot(xt[...], columns(recv, D + COLS * n, COLS), ((1,), (1,)), HIGHEST) for n in range(2)]
    low = [part.astype(f32) for part in split(jnp.concatenate(low, axis=1))[0:2]]
    rows = [slice(4 * g, 4 * g + 4) for g in range(GAMES)]
    queries = [heads[j][r] for r in rows for j in range(2)]
    for d in range(N):
        own = rows[d % 4]
        piece = queries + [part[own] for part in low]
        out[PLACE[d]] = jnp.concatenate(piece, axis=0).astype(bf16)


def fresh_pair(recv, base, up, gains, cos4, sin4, t):
    total = recv[0, 32:40, :].astype(f32)
    for s in range(1, N):
        total += recv[s, 32:40, :].astype(f32)
    low = total[0:4] + total[4:8]
    low = jnp.concatenate([low, jnp.zeros((4, 128), f32)], axis=0)
    sums = jnp.concatenate([base[...], jnp.zeros((4, 256), f32)], axis=0)
    keys = sums[:, 0:128] + 2.0 * dot(low[:, 0:64], up[0], precision=HIGHEST)
    values = sums[:, 128:256] + 2.0 * dot(low[:, 64:128], up[1], precision=HIGHEST)
    game = lax.rem(t, 4)
    zeros = jnp.zeros((4, HD), f32)
    cosine = jnp.concatenate([cos4[game], zeros], axis=0)
    sine = jnp.concatenate([sin4[game], zeros], axis=0)
    keys = rotate(head_norm(keys, gains[1:2, :]), cosine, sine)
    return keys, values


def softmax(scores, valid):
    scores = jnp.where(valid, scores * score_scale, masked_score)
    peak = jnp.max(scores, axis=-1, keepdims=True)
    weights = jnp.where(valid, jnp.exp(scores - peak), 0.0)
    return peak, jnp.sum(weights, axis=-1, keepdims=True), weights.astype(bf16)


def as_row(column, eye):
    return jnp.sum(jnp.where(eye, column, 0.0), axis=0, keepdims=True)


def attend(lengths, recv, ck, cv, base, up, gains, cos4, sin4, out, qs, ms, ls, accs):
    t = lax.axis_index("tensor")
    fk, fv = fresh_pair(recv, base, up, gains, cos4, sin4, t)
    slot = t * BLOCK + lax.broadcasted_iota(jnp.int32, (1, BLOCK), 1)
    pairs = [(k, g) for k in range(KVH) for g in range(GAMES)]
    lanes = [slice(HD * k, HD * k + HD) for k in range(KVH)]
    wide = [recv[PLACE[s], 0:32, :].astype(f32) for s in range(N)]
    scores = []
    for k, g in pairs:
        rows = slice(8 * g, 8 * g + 8)
        q = jnp.concatenate([w[rows] for w in wide[4 * k : 4 * k + 4]], axis=0).astype(bf16)
        qs[4 * k + g] = q
        scores.append(dot(q, ck[g, :, lanes[k]], ((1,), (1,))))
    valid = [jnp.broadcast_to(slot < lengths[g], (32, BLOCK)) for g in range(GAMES)]
    valid = jnp.concatenate(valid * KVH, axis=0)
    peak, total, weights = softmax(jnp.concatenate(scores, axis=0), valid)
    for n, (k, g) in enumerate(pairs):
        rows = slice(32 * n, 32 * n + 32)
        ms[n] = peak[rows]
        ls[n] = total[rows]
        accs[n] = dot(weights[rows], cv[g, :, lanes[k]])
    zeros = jnp.zeros((120, HD), f32)
    keys = jnp.concatenate([fk, zeros], axis=0).astype(bf16)
    values = jnp.concatenate([fv, zeros], axis=0).astype(bf16)
    step = lax.rem(lax.broadcasted_iota(jnp.int32, (32, HD), 0), 4)
    causal = lax.broadcasted_iota(jnp.int32, (32, HD), 1) <= step
    fresh_peak, fresh_sum, fresh_weights = softmax(dot(qs[t], keys, ((1,), (1,))), causal)
    fresh_acc = dot(fresh_weights, values)
    highest = jnp.maximum(ms[t], fresh_peak)
    old, new = jnp.exp(ms[t] - highest), jnp.exp(fresh_peak - highest)
    ls[t] = ls[t] * old + fresh_sum * new
    accs[t] = accs[t] * old + fresh_acc * new
    ms[t] = highest
    ones = [lax.broadcasted_iota(jnp.int32, (128, 128), n) for n in range(2)]
    eye = ones[0] == ones[1]
    order = [(i, g) for i in range(4) for g in range(GAMES)]
    for k in range(KVH):
        stats = []
        for ref in (ms, ls):
            column = [ref[4 * k + g, 8 * i : 8 * i + 8, :] for i, g in order]
            row = as_row(jnp.concatenate(column, axis=0), eye)
            stats += [part.astype(f32) for part in split(row)]
        stats = jnp.concatenate(stats + [jnp.zeros((2, 128), f32)], axis=0)
        for i in range(4):
            mine = [accs[4 * k + g, 8 * i : 8 * i + 8, :] for g in range(GAMES)]
            own = pltpu.roll(stats, 128 - 32 * i, 1) if i else stats
            piece = jnp.concatenate(mine + [own], axis=0)
            out[PLACE[4 * k + i]] = piece.astype(bf16)


def project(recv, ow, od, out):
    tails = [recv[s, 32:40, :].astype(f32) for s in range(N)]
    peaks = jnp.concatenate([p[0:1] + p[1:2] + p[2:3] for p in tails], axis=0)
    sums = jnp.concatenate([p[3:4] + p[4:5] + p[5:6] for p in tails], axis=0)
    highest = jnp.max(peaks, axis=0, keepdims=True)
    scale = jnp.exp(peaks - highest)
    total = jnp.sum(sums * scale, axis=0, keepdims=True)
    share = scale / total
    share = jnp.concatenate([share, jnp.zeros((112, 128), f32)], axis=0).T
    acc = jnp.zeros((32, HD), f32)
    for s in range(N):
        acc += recv[s, 0:32, :].astype(f32) * share[0:32, s : s + 1]
    halves = [
        jnp.concatenate([acc[8 * g + 4 * j : 8 * g + 4 * j + 4] for g in range(GAMES)], axis=0)
        for j in range(2)
    ]
    attended = jnp.concatenate(halves, axis=1).astype(bf16)
    low = dot(attended.astype(f32), od[...], ((1,), (1,)), HIGHEST)
    for p in range(N // 2):
        part = dot(attended, ow[:, 640 * p : 640 * p + 640])
        out[PLACE[2 * p]] = jnp.concatenate([part[:, 0:COLS], low], axis=1).astype(bf16)
        out[PLACE[2 * p + 1]] = jnp.concatenate([part[:, COLS:640], low], axis=1).astype(bf16)


def add_residual(recv, ou, st, out):
    total = recv[0].astype(f32)
    for s in range(1, N):
        total += recv[s].astype(f32)
    projected = total[:, 0:COLS] + 2.0 * dot(total[:, COLS:WIDE], ou[...], precision=HIGHEST)
    stream = st[...] + projected
    tail = jnp.concatenate([stream[0:8, 256:COLS], stream[8:16, 256:COLS]], axis=1)
    piece = jnp.concatenate([stream[:, 0:128], stream[:, 128:256], tail], axis=0).astype(bf16)
    for d in range(N):
        out[d] = piece


def finish(recv, gain, residual, normed, stream):
    squares = jnp.zeros((ROWS, 128), f32)
    for p in range(N // 2):
        parts = []
        for s in (2 * p, 2 * p + 1):
            whole = recv[PLACE[s]].astype(f32)
            tail = whole[32:40]
            parts += [whole[0:16], whole[16:32]]
            parts.append(jnp.concatenate([tail[:, 0:64], tail[:, 64:128]], axis=0))
        both = jnp.concatenate(parts, axis=1)
        stream[:, 640 * p : 640 * p + 640] = both
        for c in range(5):
            squares += both[:, 128 * c : 128 * c + 128] ** 2
    mean = jnp.sum(squares, axis=-1, keepdims=True) * (1.0 / D)
    scale = lax.rsqrt(mean + epsilon)
    gains = gain[...].astype(f32)
    for p in range(N // 2):
        lanes = slice(640 * p, 640 * p + 640)
        both = stream[:, lanes]
        own = jnp.concatenate([gains[5 * p + c : 5 * p + c + 1, :] for c in range(5)], axis=1)
        scaled = both * scale * own
        for g in range(GAMES):
            rows = slice(4 * g, 4 * g + 4)
            residual[g, :, lanes] = both[rows].astype(bf16)
            normed[g, :, lanes] = scaled[rows].astype(bf16)


def exchange(array, axis):
    groups = [ORDER] if axis == "tensor" else None
    return lax.all_to_all(array, axis, 0, 0, tiled=True, axis_index_groups=groups)


def rope_tables(lengths):
    positions = lengths[:, None] + jnp.arange(STEPS, dtype=jnp.int32)[None, :]
    inverse = rope_theta ** (-(jnp.arange(HD // 2, dtype=f32) * 2.0 / HD))
    angles = positions.astype(f32)[..., None] * inverse
    cos, sin = jnp.cos(angles), jnp.sin(angles)
    return jnp.concatenate([cos, cos], axis=-1), jnp.concatenate([-sin, sin], axis=-1)


def local(
    states,
    input_gain,
    post_gain,
    norm_gains,
    query_weight,
    key_value_weight,
    output_weight,
    query_down,
    query_up,
    pair_down,
    pair_up,
    output_down,
    output_up,
    cache_keys,
    cache_values,
    lengths,
):
    shape = jax.ShapeDtypeStruct
    cos, sin = rope_tables(lengths)
    dma = pltpu.SemaphoreType.DMA
    shared, x, own_x, own_states = run(
        prepare,
        (
            shape((N, 4, 640), f32),
            shape((ROWS, D), bf16),
            shape((ROWS, COLS), f32),
            shape((ROWS, COLS), f32),
        ),
        (
            query_down.T,
            pair_up,
            states,
            key_value_weight,
            input_gain.reshape(D // 128, 128),
        ),
        "prepare",
        specs=[HBM] * 5,
        limit=60 << 20,
        scratch=[
            pltpu.VMEM((4, COLS), f32),
            pltpu.VMEM((2, 4, 32), f32),
            pltpu.VMEM((GAMES, STEPS, D), bf16),
            pltpu.VMEM((2, COLS, 512), bf16),
            pltpu.VMEM((D // 128, 128), bf16),
            pltpu.VMEM((ROWS, D), f32),
            pltpu.VMEM((ROWS, 1024), f32),
            dma((5,)),
        ],
    )
    own = jnp.concatenate(
        [
            pair_down[0].T,
            pair_down[1].T,
            query_up,
            output_down.T,
            output_up,
            jnp.zeros((4, 64), f32),
        ],
        axis=1,
    )
    shared, own, cos, sin, query_turned = lax.optimization_barrier(
        (exchange(shared, "tensor"), own, cos, sin, query_weight.T)
    )
    factors, base = run(
        regroup,
        (shape((N, 4, HALF), f32), shape((4, 256), f32)),
        (shared, own),
        "regroup",
        scratch=[pltpu.VMEM((4, FULL), f32)],
    )
    factors = exchange(factors, "group")
    factors = run(assemble, shape((2, RANK, HALF), f32), (factors,), "assemble")
    pairs = [[2 * i, 2 * i + 1] for i in range(N // 2)]
    factors = lax.all_to_all(factors, "group", 0, 0, tiled=True, axis_index_groups=pairs)
    queries, down_output, up_output, up_pair = run(
        merge_queries,
        (
            shape((N, 40, HD), bf16),
            shape((RANK, 256), f32),
            shape((RANK, COLS), f32),
            shape((2, RANK, HD), f32),
        ),
        (factors, query_turned, x, own_x, norm_gains, cos, sin),
        "merge_queries",
    )
    queries = exchange(queries, "tensor")
    partials = run(
        attend,
        shape((N, 40, HD), bf16),
        (
            lengths,
            queries,
            cache_keys,
            cache_values,
            base,
            up_pair,
            norm_gains,
            cos,
            sin,
        ),
        "attend",
        specs=[SMEM] + [VMEM] * 8,
        scratch=[
            pltpu.VMEM((N, 32, HD), bf16),
            pltpu.VMEM((N, 32, 1), f32),
            pltpu.VMEM((N, 32, 1), f32),
            pltpu.VMEM((N, 32, HD), f32),
        ],
    )
    partials = exchange(partials, "tensor")
    projected = run(
        project, shape((N, ROWS, WIDE), bf16), (partials, output_weight, down_output), "project"
    )
    projected = exchange(projected, "tensor")
    pieces = run(
        add_residual,
        shape((N, 40, HD), bf16),
        (projected, up_output, own_states),
        "add_residual",
    )
    pieces = exchange(pieces, "tensor")
    return run(
        finish,
        (shape((GAMES, STEPS, D), bf16), shape((GAMES, STEPS, D), bf16)),
        (pieces, post_gain.reshape(D // 128, 128)),
        "finish",
        scratch=[pltpu.VMEM((ROWS, D), f32)],
    )


def solution(mesh):
    in_specs = (
        P("group", None, None),
        P(),
        P(),
        P(),
        P(None, "tensor"),
        P(None, "tensor", None),
        P("tensor", None),
        P("tensor", "group"),
        P("group", "tensor"),
        P(None, "tensor", "group"),
        P(None, "group", "tensor"),
        P("tensor", "group"),
        P("group", "tensor"),
        P("group", "tensor", None),
        P("group", "tensor", None),
        P("group"),
    )
    out_specs = (P("group", None, None), P("group", None, None))
    return jax.shard_map(local, mesh=mesh, in_specs=in_specs, out_specs=out_specs, check_vma=False)
```

```python
import functools
import math

import jax
import jax.numpy as jnp
from jax import lax
from jax.experimental import pallas as pl
from jax.experimental.pallas import tpu as pltpu
from jax.sharding import PartitionSpec as P

HD = 128
QH = 32
KVH = 4
N = 16
ROWS = 16
GAMES = 4
STEPS = 4
RANK = 64
D = 5120
COLS = D // N
ORDER = [t for first in (0, 2, 1, 3) for t in range(first, N, 4)]
PLACE = [ORDER.index(t) for t in range(N)]
WIDE = COLS + RANK
BLOCK = 256
FULL = D + 1792
HALF = FULL // 2

epsilon = 1e-06
rope_theta = 1000000.0
masked_score = -1e30
score_scale = 1.0 / math.sqrt(HD)
HIGHEST = lax.Precision.HIGHEST
f32 = jnp.float32
bf16 = jnp.bfloat16

VMEM = pl.BlockSpec(memory_space=pltpu.VMEM)
SMEM = pl.BlockSpec(memory_space=pltpu.SMEM)
HBM = pl.BlockSpec(memory_space=pltpu.HBM)


def dot(a, b, contract=((1,), (0,)), precision=None):
    return lax.dot_general(
        a, b, (contract, ((), ())), precision=precision, preferred_element_type=f32
    )


def run(body, outs, args, name, specs=None, scratch=(), limit=48 << 20):
    return pl.pallas_call(
        body,
        out_shape=outs,
        in_specs=specs or [VMEM] * len(args),
        out_specs=jax.tree.map(lambda _: VMEM, outs),
        scratch_shapes=list(scratch),
        compiler_params=pltpu.CompilerParams(vmem_limit_bytes=limit),
        name=name,
    )(*args)


def copies(pairs, sems):
    started = [pltpu.make_async_copy(src, dst, sems.at[i]) for i, (src, dst) in enumerate(pairs)]
    for copy in started:
        copy.start()
    return started


def own_columns(ref, t):
    odd = lax.rem(t, 2)
    start = pl.multiple_of(t * COLS - odd * 64, 128)
    window = ref[:, pl.ds(start, WIDE)]
    return jnp.where(odd == 1, window[:, 64:WIDE], window[:, 0:COLS])


def prepare(
    qd_hbm, pu_hbm, states_hbm, kvw_hbm, gain_hbm, out, x_out, xt_out, st_out,
    qd, pu, states, kvw, gain, act, part, sems,
):
    waits = copies(
        [
            (states_hbm, states),
            (gain_hbm, gain),
            (kvw_hbm, kvw),
            (qd_hbm, qd),
            (pu_hbm, pu),
        ],
        sems,
    )
    t = lax.axis_index("tensor")
    waits[0].wait()
    for g in range(GAMES):
        act[4 * g : 4 * g + 4, :] = states[g].astype(f32)
    st_out[...] = own_columns(act, t)
    values = act[...]
    scale = lax.rsqrt(jnp.mean(values * values, axis=-1, keepdims=True) + epsilon)
    waits[1].wait()
    gains = gain[...].astype(f32)
    for c in range(D // 128):
        lanes = slice(128 * c, 128 * c + 128)
        x = (values[:, lanes] * scale * gains[c : c + 1, :]).astype(bf16)
        x_out[:, lanes] = x
        act[:, lanes] = x.astype(f32)
    xt = own_columns(act, t)
    xt_out[...] = xt
    waits[2].wait()
    for n in range(2):
        part[:, 512 * n : 512 * n + 512] = dot(xt.astype(bf16), kvw[n])
    for copy in waits[3:]:
        copy.wait()
    shared = jnp.concatenate([qd[...], pu[0], pu[1]], axis=1)
    for d in range(N):
        k, g = d // 4, d % 4
        rows = slice(4 * g, 4 * g + 4)
        out[PLACE[d], :, 0:WIDE] = shared
        out[PLACE[d], :, WIDE : WIDE + 128] = part[rows, 128 * k : 128 * k + 128]
        out[PLACE[d], :, WIDE + 128 : 640] = part[rows, 512 + 128 * k : 640 + 128 * k]


def regroup(recv, own, out, base_out, line):
    t = lax.axis_index("tensor")
    base = recv[0, :, WIDE:640]
    for s in range(1, N):
        base += recv[s, :, WIDE:640]
    base_out[...] = base
    for p in range(N // 2):
        line[:, 640 * p : 640 * p + 640] = jnp.concatenate(
            [recv[PLACE[2 * p + c], 0:4, 0:COLS] for c in range(2)], axis=1
        )
    line[:, D : D + 1536] = own[...]
    pairs = [recv[t // 4 + PLACE[c], 0:4, COLS:WIDE] for c in range(4)]
    line[:, D + 1536 : FULL] = jnp.concatenate(
        [c[:, 32 * n : 32 * n + 32] for n in range(2) for c in pairs], axis=1
    )
    for d in range(N):
        out[d] = line[:, HALF * (d % 2) : HALF * (d % 2) + HALF]


def assemble(recv, out):
    for c in range(2):
        for g in range(N):
            out[c, 4 * g : 4 * g + 4, :] = recv[g]


def columns(recv, start, width):
    if start + width <= HALF:
        return recv[0, :, start : start + width]
    if start >= HALF:
        return recv[1, :, start - HALF : start - HALF + width]
    left = recv[0, :, start:HALF]
    return jnp.concatenate([left, recv[1, :, 0 : start + width - HALF]], axis=1)


def rotate(values, cosine, sine):
    return values * cosine + pltpu.roll(values, HD // 2, 1) * sine


def head_norm(values, gain):
    return values * lax.rsqrt(jnp.mean(values * values, axis=-1, keepdims=True) + epsilon) * gain


def split(values):
    high = values.astype(bf16)
    rest = values - high.astype(f32)
    middle = rest.astype(bf16)
    return high, middle, (rest - middle.astype(f32)).astype(bf16)


def merge_queries(recv, qwt, x, xt, gains, cos, sin, out, od_out, ou_out, up_out):
    od_out[...] = columns(recv, 6016, 256)
    ou_out[...] = columns(recv, 6272, COLS)
    for n in range(2):
        up_out[n] = columns(recv, 6656 + 128 * n, 128)
    uh, um, ul = [u.astype(f32) for u in split(columns(recv, 5760, 256))]
    ups = jnp.concatenate([uh, uh, um, um, ul, uh], axis=0).T.astype(bf16)
    raw = jnp.zeros((ROWS, 256), f32)
    for p in range(N // 2):
        lanes = slice(640 * p, 640 * p + 640)
        h, m, l = split(columns(recv, 640 * p, 640))
        update = dot(ups, jnp.concatenate([h, m, h, m, h, l], axis=0))
        merged = (qwt[:, lanes].astype(f32) + 2.0 * update).astype(bf16)
        raw += dot(x[:, lanes], merged, ((1,), (1,)))
    cosine = jnp.concatenate([cos[g] for g in range(GAMES)], axis=0)
    sine = jnp.concatenate([sin[g] for g in range(GAMES)], axis=0)
    heads = []
    for h in range(2):
        v = head_norm(raw[:, HD * h : HD * h + HD], gains[0:1, :])
        heads.append(rotate(v, cosine, sine))
    low = [dot(xt[...], columns(recv, D + COLS * n, COLS), ((1,), (1,)), HIGHEST) for n in range(2)]
    low = [part.astype(f32) for part in split(jnp.concatenate(low, axis=1))[0:2]]
    rows = [slice(4 * g, 4 * g + 4) for g in range(GAMES)]
    queries = [heads[j][r] for r in rows for j in range(2)]
    for d in range(N):
        own = rows[d % 4]
        piece = queries + [part[own] for part in low]
        out[PLACE[d]] = jnp.concatenate(piece, axis=0).astype(bf16)


def fresh_pair(recv, base, up, gains, cos4, sin4, t):
    total = recv[0, 32:40, :].astype(f32)
    for s in range(1, N):
        total += recv[s, 32:40, :].astype(f32)
    low = total[0:4] + total[4:8]
    low = jnp.concatenate([low, jnp.zeros((4, 128), f32)], axis=0)
    sums = jnp.concatenate([base[...], jnp.zeros((4, 256), f32)], axis=0)
    keys = sums[:, 0:128] + 2.0 * dot(low[:, 0:64], up[0], precision=HIGHEST)
    values = sums[:, 128:256] + 2.0 * dot(low[:, 64:128], up[1], precision=HIGHEST)
    game = lax.rem(t, 4)
    zeros = jnp.zeros((4, HD), f32)
    cosine = jnp.concatenate([cos4[game], zeros], axis=0)
    sine = jnp.concatenate([sin4[game], zeros], axis=0)
    keys = rotate(head_norm(keys, gains[1:2, :]), cosine, sine)
    return keys, values


def softmax(scores, valid):
    scores = jnp.where(valid, scores * score_scale, masked_score)
    peak = jnp.max(scores, axis=-1, keepdims=True)
    weights = jnp.where(valid, jnp.exp(scores - peak), 0.0)
    return peak, jnp.sum(weights, axis=-1, keepdims=True), weights.astype(bf16)


def as_row(column, eye):
    return jnp.sum(jnp.where(eye, column, 0.0), axis=0, keepdims=True)


def attend(lengths, recv, ck, cv, base, up, gains, cos4, sin4, out, qs, ms, ls, accs):
    t = lax.axis_index("tensor")
    fk, fv = fresh_pair(recv, base, up, gains, cos4, sin4, t)
    slot = t * BLOCK + lax.broadcasted_iota(jnp.int32, (1, BLOCK), 1)
    pairs = [(k, g) for k in range(KVH) for g in range(GAMES)]
    lanes = [slice(HD * k, HD * k + HD) for k in range(KVH)]
    wide = [recv[PLACE[s], 0:32, :].astype(f32) for s in range(N)]
    scores = []
    for k, g in pairs:
        rows = slice(8 * g, 8 * g + 8)
        q = jnp.concatenate([w[rows] for w in wide[4 * k : 4 * k + 4]], axis=0).astype(bf16)
        qs[4 * k + g] = q
        scores.append(dot(q, ck[g, :, lanes[k]], ((1,), (1,))))
    valid = [jnp.broadcast_to(slot < lengths[g], (32, BLOCK)) for g in range(GAMES)]
    valid = jnp.concatenate(valid * KVH, axis=0)
    peak, total, weights = softmax(jnp.concatenate(scores, axis=0), valid)
    for n, (k, g) in enumerate(pairs):
        rows = slice(32 * n, 32 * n + 32)
        ms[n] = peak[rows]
        ls[n] = total[rows]
        accs[n] = dot(weights[rows], cv[g, :, lanes[k]])
    zeros = jnp.zeros((120, HD), f32)
    keys = jnp.concatenate([fk, zeros], axis=0).astype(bf16)
    values = jnp.concatenate([fv, zeros], axis=0).astype(bf16)
    step = lax.rem(lax.broadcasted_iota(jnp.int32, (32, HD), 0), 4)
    causal = lax.broadcasted_iota(jnp.int32, (32, HD), 1) <= step
    fresh_peak, fresh_sum, fresh_weights = softmax(dot(qs[t], keys, ((1,), (1,))), causal)
    fresh_acc = dot(fresh_weights, values)
    highest = jnp.maximum(ms[t], fresh_peak)
    old, new = jnp.exp(ms[t] - highest), jnp.exp(fresh_peak - highest)
    ls[t] = ls[t] * old + fresh_sum * new
    accs[t] = accs[t] * old + fresh_acc * new
    ms[t] = highest
    ones = [lax.broadcasted_iota(jnp.int32, (128, 128), n) for n in range(2)]
    eye = ones[0] == ones[1]
    order = [(i, g) for i in range(4) for g in range(GAMES)]
    for k in range(KVH):
        stats = []
        for ref in (ms, ls):
            column = [ref[4 * k + g, 8 * i : 8 * i + 8, :] for i, g in order]
            row = as_row(jnp.concatenate(column, axis=0), eye)
            stats += [part.astype(f32) for part in split(row)]
        stats = jnp.concatenate(stats + [jnp.zeros((2, 128), f32)], axis=0)
        for i in range(4):
            mine = [accs[4 * k + g, 8 * i : 8 * i + 8, :] for g in range(GAMES)]
            own = pltpu.roll(stats, 128 - 32 * i, 1) if i else stats
            piece = jnp.concatenate(mine + [own], axis=0)
            out[PLACE[4 * k + i]] = piece.astype(bf16)


def project(recv, ow, od, out):
    tails = [recv[s, 32:40, :].astype(f32) for s in range(N)]
    peaks = jnp.concatenate([p[0:1] + p[1:2] + p[2:3] for p in tails], axis=0)
    sums = jnp.concatenate([p[3:4] + p[4:5] + p[5:6] for p in tails], axis=0)
    highest = jnp.max(peaks, axis=0, keepdims=True)
    scale = jnp.exp(peaks - highest)
    total = jnp.sum(sums * scale, axis=0, keepdims=True)
    share = scale / total
    share = jnp.concatenate([share, jnp.zeros((112, 128), f32)], axis=0).T
    acc = jnp.zeros((32, HD), f32)
    for s in range(N):
        acc += recv[s, 0:32, :].astype(f32) * share[0:32, s : s + 1]
    halves = [
        jnp.concatenate([acc[8 * g + 4 * j : 8 * g + 4 * j + 4] for g in range(GAMES)], axis=0)
        for j in range(2)
    ]
    attended = jnp.concatenate(halves, axis=1).astype(bf16)
    low = dot(attended.astype(f32), od[...], ((1,), (1,)), HIGHEST)
    for p in range(N // 2):
        part = dot(attended, ow[:, 640 * p : 640 * p + 640])
        out[PLACE[2 * p]] = jnp.concatenate([part[:, 0:COLS], low], axis=1).astype(bf16)
        out[PLACE[2 * p + 1]] = jnp.concatenate([part[:, COLS:640], low], axis=1).astype(bf16)


def add_residual(recv, ou, st, out):
    total = recv[0].astype(f32)
    for s in range(1, N):
        total += recv[s].astype(f32)
    projected = total[:, 0:COLS] + 2.0 * dot(total[:, COLS:WIDE], ou[...], precision=HIGHEST)
    stream = st[...] + projected
    tail = jnp.concatenate([stream[0:8, 256:COLS], stream[8:16, 256:COLS]], axis=1)
    piece = jnp.concatenate([stream[:, 0:128], stream[:, 128:256], tail], axis=0).astype(bf16)
    for d in range(N):
        out[d] = piece


def finish(recv, gain, residual, normed, stream):
    squares = jnp.zeros((ROWS, 128), f32)
    for p in range(N // 2):
        parts = []
        for s in (2 * p, 2 * p + 1):
            whole = recv[PLACE[s]].astype(f32)
            tail = whole[32:40]
            parts += [whole[0:16], whole[16:32]]
            parts.append(jnp.concatenate([tail[:, 0:64], tail[:, 64:128]], axis=0))
        both = jnp.concatenate(parts, axis=1)
        stream[:, 640 * p : 640 * p + 640] = both
        for c in range(5):
            squares += both[:, 128 * c : 128 * c + 128] ** 2
    mean = jnp.sum(squares, axis=-1, keepdims=True) * (1.0 / D)
    scale = lax.rsqrt(mean + epsilon)
    gains = gain[...].astype(f32)
    for p in range(N // 2):
        lanes = slice(640 * p, 640 * p + 640)
        both = stream[:, lanes]
        own = jnp.concatenate([gains[5 * p + c : 5 * p + c + 1, :] for c in range(5)], axis=1)
        scaled = both * scale * own
        for g in range(GAMES):
            rows = slice(4 * g, 4 * g + 4)
            residual[g, :, lanes] = both[rows].astype(bf16)
            normed[g, :, lanes] = scaled[rows].astype(bf16)


def exchange(array, axis):
    groups = [ORDER] if axis == "tensor" else None
    return lax.all_to_all(array, axis, 0, 0, tiled=True, axis_index_groups=groups)


def rope_tables(lengths):
    positions = lengths[:, None] + jnp.arange(STEPS, dtype=jnp.int32)[None, :]
    inverse = rope_theta ** (-(jnp.arange(HD // 2, dtype=f32) * 2.0 / HD))
    angles = positions.astype(f32)[..., None] * inverse
    cos, sin = jnp.cos(angles), jnp.sin(angles)
    return jnp.concatenate([cos, cos], axis=-1), jnp.concatenate([-sin, sin], axis=-1)


def local(
    states,
    input_gain,
    post_gain,
    norm_gains,
    query_weight,
    key_value_weight,
    output_weight,
    query_down,
    query_up,
    pair_down,
    pair_up,
    output_down,
    output_up,
    cache_keys,
    cache_values,
    lengths,
):
    shape = jax.ShapeDtypeStruct
    cos, sin = rope_tables(lengths)
    dma = pltpu.SemaphoreType.DMA
    shared, x, own_x, own_states = run(
        prepare,
        (
            shape((N, 4, 640), f32),
            shape((ROWS, D), bf16),
            shape((ROWS, COLS), f32),
            shape((ROWS, COLS), f32),
        ),
        (
            query_down.T,
            pair_up,
            states,
            key_value_weight,
            input_gain.reshape(D // 128, 128),
        ),
        "prepare",
        specs=[HBM] * 5,
        limit=60 << 20,
        scratch=[
            pltpu.VMEM((4, COLS), f32),
            pltpu.VMEM((2, 4, 32), f32),
            pltpu.VMEM((GAMES, STEPS, D), bf16),
            pltpu.VMEM((2, COLS, 512), bf16),
            pltpu.VMEM((D // 128, 128), bf16),
            pltpu.VMEM((ROWS, D), f32),
            pltpu.VMEM((ROWS, 1024), f32),
            dma((5,)),
        ],
    )
    own = jnp.concatenate(
        [
            pair_down[0].T,
            pair_down[1].T,
            query_up,
            output_down.T,
            output_up,
            jnp.zeros((4, 64), f32),
        ],
        axis=1,
    )
    shared, own, cos, sin, query_turned = lax.optimization_barrier(
        (exchange(shared, "tensor"), own, cos, sin, query_weight.T)
    )
    factors, base = run(
        regroup,
        (shape((N, 4, HALF), f32), shape((4, 256), f32)),
        (shared, own),
        "regroup",
        scratch=[pltpu.VMEM((4, FULL), f32)],
    )
    factors = exchange(factors, "group")
    factors = run(assemble, shape((2, RANK, HALF), f32), (factors,), "assemble")
    pairs = [[2 * i, 2 * i + 1] for i in range(N // 2)]
    factors = lax.all_to_all(factors, "group", 0, 0, tiled=True, axis_index_groups=pairs)
    queries, down_output, up_output, up_pair = run(
        merge_queries,
        (
            shape((N, 40, HD), bf16),
            shape((RANK, 256), f32),
            shape((RANK, COLS), f32),
            shape((2, RANK, HD), f32),
        ),
        (factors, query_turned, x, own_x, norm_gains, cos, sin),
        "merge_queries",
    )
    queries = exchange(queries, "tensor")
    partials = run(
        attend,
        shape((N, 40, HD), bf16),
        (
            lengths,
            queries,
            cache_keys,
            cache_values,
            base,
            up_pair,
            norm_gains,
            cos,
            sin,
        ),
        "attend",
        specs=[SMEM] + [VMEM] * 8,
        scratch=[
            pltpu.VMEM((N, 32, HD), bf16),
            pltpu.VMEM((N, 32, 1), f32),
            pltpu.VMEM((N, 32, 1), f32),
            pltpu.VMEM((N, 32, HD), f32),
        ],
    )
    partials = exchange(partials, "tensor")
    projected = run(
        project, shape((N, ROWS, WIDE), bf16), (partials, output_weight, down_output), "project"
    )
    projected = exchange(projected, "tensor")
    pieces = run(
        add_residual,
        shape((N, 40, HD), bf16),
        (projected, up_output, own_states),
        "add_residual",
    )
    pieces = exchange(pieces, "tensor")
    return run(
        finish,
        (shape((GAMES, STEPS, D), bf16), shape((GAMES, STEPS, D), bf16)),
        (pieces, post_gain.reshape(D // 128, 128)),
        "finish",
        scratch=[pltpu.VMEM((ROWS, D), f32)],
    )


def solution(mesh):
    in_specs = (
        P("group", None, None),
        P(),
        P(),
        P(),
        P(None, "tensor"),
        P(None, "tensor", None),
        P("tensor", None),
        P("tensor", "group"),
        P("group", "tensor"),
        P(None, "tensor", "group"),
        P(None, "group", "tensor"),
        P("tensor", "group"),
        P("group", "tensor"),
        P("group", "tensor", None),
        P("group", "tensor", None),
        P("group"),
    )
    out_specs = (P("group", None, None), P("group", None, None))
    return jax.shard_map(local, mesh=mesh, in_specs=in_specs, out_specs=out_specs, check_vma=False)
```
